32 devices in a mesh: org: 8 (over y, x, core), dst: 4 (over z).
Axes of the slice: x: 2, y: 2, z: 4, core: 2. Of those that a mesh axis runs over, the one named last changes fastest.
Arguments:
- counts: int32 [8, 4096, 4096], P(None, 'org', 'dst'), may hold values from 0 to 127, as said below
- block_scales: float32 [8, 32, 32], P(None, 'org', 'dst'), may hold values from 0.05 to 12.5, as said below
- anchor_factor: float32 [64, 4096], P(None, 'org'), may hold values from 0.2 to 9, as said below
- dest_factor: float32 [64, 4096], P(None, 'dst'), may hold values from 0.2 to 9, as said below
- hour_factor: float32 [8, 64], replicated, may hold values from 0.5 to 2
Outputs:
- anchor_updated: float32 [64, 4096], P(None, 'org')
- dest_updated: float32 [64, 4096], P(None, 'dst')
The draws below stay inside these ranges and needn't reach their ends.
Inputs may be any that keep to these rules, and one draw needn't show every extreme that they name: Whole trip counts. `block_scales`: positive. `anchor_factor`: positive. `dest_factor`: positive.
All inputs are finite; a program needn't handle non-finite values.
Results may differ from the reference program's by a relative error of at most 0.0003.
Values sent between devices are 32-bit elements; how exact they have to be, the bound alone decides.
No kernel may reach another device: no remote copies, remote signals or barrier semaphores. Data moves between devices by JAX's collectives and lax.ppermute only.
A program may use at most 128 MiB of HBM per device.

```python
import math
import jax
import jax.numpy as jnp
from jax import lax

RANK = 64
HOURS = 8
SCALE_BLOCK = 128
SWEEPS = 6
ANCHORS = 4096
DESTINATIONS = 4096


def ramp_factor(key, length, growth, low_end, high_end):
    uniform_part = jax.random.uniform(key, (RANK, length), jnp.float32, low_end, high_end)
    position = jnp.arange(length, dtype=jnp.float32) / (length - 1)
    return uniform_part * jnp.exp(jnp.log(growth) * position)


def draw_counts(key, part):
    components = 4
    folded = jax.random.fold_in(key, 51)
    anchor_key = jax.random.fold_in(folded, 1)
    dest_key = jax.random.fold_in(folded, 2)
    hour_key = jax.random.fold_in(folded, 3)
    jitter_key = jax.random.fold_in(folded, 4)
    anchor_mass = jax.random.randint(anchor_key, (components, ANCHORS), 0, 8, jnp.int32).at[:, 0].set(7)
    dest_mass = jax.random.randint(dest_key, (components, DESTINATIONS), 0, 8, jnp.int32).at[:, 0].set(7)
    hour_mass = jax.random.randint(hour_key, (HOURS, components), 1, 4, jnp.int32).at[0, :].set(3)
    weighted = hour_mass[:, :, None] * anchor_mass[None, :, :]
    structure = jnp.einsum('hki,kj->hij', weighted, dest_mass)
    jitter_part = jax.random.randint(jitter_key, (HOURS, ANCHORS, DESTINATIONS), 0, 32, jnp.int32)
    return jnp.clip(structure // 2 + jitter_part, 0, 127).astype(jnp.int32)


def draw_anchor_factor(key, part):
    folded = jax.random.fold_in(key, 11)
    return ramp_factor(folded, ANCHORS, 3.0, 0.5, 1.5)


def draw_dest_factor(key, part):
    folded = jax.random.fold_in(key, 37)
    return ramp_factor(folded, DESTINATIONS, 3.0, 0.5, 1.5)


def draw_block_scales(key, part):
    row_blocks = ANCHORS // SCALE_BLOCK
    col_blocks = DESTINATIONS // SCALE_BLOCK
    folded = jax.random.fold_in(key, 23)
    unit_draw = jax.random.uniform(folded, (HOURS, row_blocks, col_blocks), jnp.float32)
    low_end = 0.1
    high_end = 1.0
    growth = 3.0
    levels = jnp.exp(jnp.log(low_end) + unit_draw * jnp.log(high_end / low_end))
    row_pos = jnp.arange(row_blocks, dtype=jnp.float32) / (row_blocks - 1)
    col_pos = jnp.arange(col_blocks, dtype=jnp.float32) / (col_blocks - 1)
    ramp_both = jnp.exp(jnp.log(growth) * (row_pos[None, :, None] + col_pos[None, None, :]))
    return levels * ramp_both


def setup_inputs(seed: int = 0) -> dict:
    streams_of = jax.random.split(jax.random.key(seed), 6)
    counts = draw_counts(jax.random.fold_in(streams_of[5], 71), 0)
    block_scales = draw_block_scales(jax.random.fold_in(streams_of[5], 71), 0)
    anchor_factor = draw_anchor_factor(jax.random.fold_in(streams_of[5], 71), 0)
    dest_factor = draw_dest_factor(jax.random.fold_in(streams_of[5], 71), 0)
    hour_factor = jnp.clip(jnp.exp(jax.random.uniform(streams_of[4], (HOURS, RANK), jnp.float32, math.log(0.5), math.log(2.0))), 0.5, 2.0)
    return {"counts": counts, "block_scales": block_scales, "anchor_factor": anchor_factor, "dest_factor": dest_factor, "hour_factor": hour_factor}


def dequantize(counts_hour, scales_hour):
    row_count, col_count = counts_hour.shape
    blocks = counts_hour.reshape(row_count // SCALE_BLOCK, SCALE_BLOCK, col_count // SCALE_BLOCK, SCALE_BLOCK).astype(jnp.float32)
    values = blocks * scales_hour[:, None, :, None]
    return values.reshape(row_count, col_count).astype(jnp.bfloat16)


def gram_matrix(factor, hour_gram):
    return jnp.dot(factor, factor.T, precision=lax.Precision.HIGHEST) * hour_gram


def update(factor, totals, gram_part):
    return factor * totals / jnp.dot(gram_part, factor, precision=lax.Precision.HIGHEST)


def reference(counts, block_scales, anchor_factor, dest_factor, hour_factor):
    tensor = jnp.stack([dequantize(counts[hour_index], block_scales[hour_index]) for hour_index in range(HOURS)])
    hour_gram = jnp.dot(hour_factor.T, hour_factor, precision=lax.Precision.HIGHEST)
    anchor_now = anchor_factor
    dest_now = dest_factor
    for sweep_index in range(SWEEPS):
        dest_low = dest_now.astype(jnp.bfloat16)
        per_hour = jnp.einsum("rj,hij->hri", dest_low, tensor, preferred_element_type=jnp.float32)
        anchor_totals = jnp.einsum("hri,hr->ri", per_hour, hour_factor, precision=lax.Precision.HIGHEST)
        anchor_now = update(anchor_now, anchor_totals, gram_matrix(dest_now, hour_gram))
        anchor_low = anchor_now.astype(jnp.bfloat16)
        per_hour = jnp.einsum("ri,hij->hrj", anchor_low, tensor, preferred_element_type=jnp.float32)
        dest_totals = jnp.einsum("hrj,hr->rj", per_hour, hour_factor, precision=lax.Precision.HIGHEST)
        dest_now = update(dest_now, dest_totals, gram_matrix(anchor_now, hour_gram))
    return (anchor_now, dest_now)
```

```python
import functools

import jax
import jax.numpy as jnp
from jax import lax
from jax.experimental import pallas as pl
from jax.experimental.pallas import tpu as pltpu
from jax.sharding import PartitionSpec as P

SCALE_BLOCK = 128
SWEEPS = 6
LANES = 128
F32 = jnp.float32
BF16 = jnp.bfloat16
HIGHEST = lax.Precision.HIGHEST

WHOLE = pl.BlockSpec(memory_space=pltpu.VMEM)
SCALAR = pl.BlockSpec(memory_space=pltpu.SMEM)
PARAMS = pltpu.CompilerParams(vmem_limit_bytes=12 * 2**20)


def in_vmem(array):
    return pltpu.with_memory_space_constraint(array, pltpu.VMEM)


def gram_rows(rank, width):
    return 8 * -(-(rank // 8) // (width // LANES))


def gram_cells(rank, width):
    per_row = width // LANES
    for block in range(rank // 8):
        yield block, rank + 8 * (block // per_row), LANES * (block % per_row)


def put_gram(message, gram):
    rank = gram.shape[0]
    width = message.shape[1]
    message[rank:, :] = jnp.zeros((message.shape[0] - rank, width), F32)
    for block, row, lane in gram_cells(rank, width):
        message[row : row + 8, lane : lane + rank] = gram[8 * block : 8 * block + 8, :]


def get_gram(message, rank):
    width = message.shape[1]
    return jnp.concatenate(
        [message[row : row + 8, lane : lane + rank] for _, row, lane in gram_cells(rank, width)], axis=0
    )


def own_gram(factor):
    return lax.dot_general(factor, factor, (((1,), (1,)), ((), ())), precision=HIGHEST, preferred_element_type=F32)


def half(ref, core, flip, size):
    start = (1 - core if flip else core) * size
    return pl.ds(pl.multiple_of(start, size), size)


def hour_sum(parts, hour_t):
    total = None
    for hour, part in enumerate(parts):
        term = part * hour_t[:, hour : hour + 1]
        total = term if total is None else total + term
    return total


def first_kernel(counts, scales, dest, hour_t, tensor, flipped, message, buffer, arrived):
    hours, rows, cols = counts.shape
    rank = dest.shape[0]
    dest_low = dest[...].astype(BF16)

    def fetch(hour, slot):
        return pltpu.make_async_copy(counts.at[hour], buffer.at[slot], arrived.at[slot])

    fetch(0, 0).start()
    fetch(1, 1).start()
    message[:rank, :] = jnp.zeros((rank, rows), F32)
    for hour in range(hours):
        slot = hour % 2
        fetch(hour, slot).wait()
        for row_block in range(rows // SCALE_BLOCK):
            row = pl.ds(row_block * SCALE_BLOCK, SCALE_BLOCK)
            for col_block in range(cols // SCALE_BLOCK):
                col = pl.ds(col_block * SCALE_BLOCK, SCALE_BLOCK)
                scale = scales[hour, row_block, col_block]
                block = (buffer[slot, row, col].astype(F32) * scale).astype(BF16)
                tensor[hour, row, col] = block
                flipped[hour, col, row] = block.T
        if hour + 2 < hours:
            fetch(hour + 2, slot).start()
        part = jnp.dot(dest_low, flipped[hour], preferred_element_type=F32)
        message[:rank, :] += part * hour_t[:, hour : hour + 1]
    put_gram(message, own_gram(dest[...]))


def anchor_kernel(core, tensor, anchor, near, far, hour_gram, hour_t, anchor_out, low_out, sent):
    rank, width = anchor.shape
    message = near[...] + far[...]
    gram_part = get_gram(message, rank) * hour_gram[...]
    low = jnp.dot(gram_part, anchor[...], precision=HIGHEST, preferred_element_type=F32)
    updated = anchor[...] * message[:rank, :] / low
    anchor_out[...] = updated
    anchor_low = updated.astype(BF16)
    low_out[...] = anchor_low
    size = tensor.shape[2] // 2
    cols = half(tensor, core[0], True, size)
    sent[:rank, :] = hour_sum(
        [jnp.dot(anchor_low, tensor[h, :, cols], preferred_element_type=F32) for h in range(tensor.shape[0])], hour_t
    )
    put_gram(sent, own_gram(updated))


def anchor_kept_kernel(core, tensor, anchor_low, hour_t, sent, kept):
    rank = anchor_low.shape[0]
    size = tensor.shape[2] // 2
    cols = half(tensor, core[0], False, size)
    low = anchor_low[...]
    kept[:rank, :] = hour_sum(
        [jnp.dot(low, tensor[h, :, cols], preferred_element_type=F32) for h in range(tensor.shape[0])], hour_t
    )
    kept[rank:, :] = sent[rank:, :]


def dest_kernel(dest, near, far, hour_gram, dest_out):
    rank = dest.shape[0]
    message = near[...] + far[...]
    gram_part = get_gram(message, rank) * hour_gram[...]
    low = jnp.dot(gram_part, dest[...], precision=HIGHEST, preferred_element_type=F32)
    dest_out[...] = dest[...] * message[:rank, :] / low


def dest_own_kernel(core, flipped, dest, hour_t, message):
    rank = dest.shape[0]
    size = flipped.shape[1] // 2
    rows = half(flipped, core[0], False, size)
    low = dest[...].astype(BF16)
    message[:rank, :] = hour_sum(
        [jnp.dot(low, flipped[h, rows, :], preferred_element_type=F32) for h in range(flipped.shape[0])], hour_t
    )
    put_gram(message, own_gram(dest[...]))


def dest_other_kernel(core, flipped, dest, hour_t, before, message):
    rank = dest.shape[0]
    size = flipped.shape[1] // 2
    rows = half(flipped, core[0], True, size)
    low = dest[...].astype(BF16)
    message[:rank, :] = before[:rank, :] + hour_sum(
        [jnp.dot(low, flipped[h, rows, :], preferred_element_type=F32) for h in range(flipped.shape[0])], hour_t
    )
    put_gram(message, own_gram(dest[...]))
    message[rank:, :] += before[rank:, :]


def call(kernel, outs, name, flops, *args):
    specs = []
    operands = []
    for arg in args:
        if arg.ndim == 1:
            specs.append(SCALAR)
            operands.append(arg)
        else:
            specs.append(WHOLE)
            operands.append(in_vmem(arg))
    result = pl.pallas_call(
        kernel,
        in_specs=specs,
        out_specs=tuple(WHOLE for _ in outs),
        out_shape=tuple(pltpu.VMEM(shape, dtype) for shape, dtype in outs),
        compiler_params=PARAMS,
        cost_estimate=pl.CostEstimate(flops=flops, bytes_accessed=0, transcendentals=0),
        name=name,
    )(*operands)
    return result if len(outs) > 1 else result[0]


def swap(array, axis, mask):
    size = lax.axis_size(axis)
    return lax.ppermute(array, axis, [(index, index ^ mask) for index in range(size)])


def sum_dest(message):
    size = lax.axis_size("dst")
    mask = 1
    while 2 * mask < size:
        message = message + swap(message, "dst", 2 * mask - 1)
        mask *= 2
    return message, swap(message, "dst", 2 * mask - 1)


def sum_anchor(message):
    size = lax.axis_size("org")
    if size == 8:
        return message + swap(message, "org", 2), swap(message, "org", 4) + swap(message, "org", 6)
    mask = 2
    while 2 * mask < size:
        message = message + swap(message, "org", mask)
        mask *= 2
    return message, swap(message, "org", mask)


def body(counts, block_scales, anchor_factor, dest_factor, hour_factor):
    hours, rows, cols = counts.shape
    rank = anchor_factor.shape[0]
    size = cols // 2
    core = lax.axis_index("org") % 2
    core_arg = core.astype(jnp.int32).reshape(1)
    hour_t = hour_factor.T
    hour_gram = jnp.dot(hour_factor.T, hour_factor, precision=HIGHEST)
    dest_rows = rank + gram_rows(rank, rows)
    anchor_rows = rank + gram_rows(rank, size)
    half_flops = 2 * 4 * hours * rank * rows * size

    tensor, flipped, message = pl.pallas_call(
        first_kernel,
        in_specs=[pl.BlockSpec(memory_space=pl.ANY), SCALAR, WHOLE, WHOLE],
        out_specs=(WHOLE, WHOLE, WHOLE),
        out_shape=(
            pltpu.VMEM((hours, rows, cols), BF16),
            pltpu.VMEM((hours, cols, rows), BF16),
            pltpu.VMEM((dest_rows, rows), F32),
        ),
        scratch_shapes=[pltpu.VMEM((2, rows, cols), jnp.int32), pltpu.SemaphoreType.DMA((2,))],
        compiler_params=PARAMS,
        name="first",
    )(
        pltpu.with_memory_space_constraint(counts, pltpu.HBM),
        block_scales,
        in_vmem(dest_factor),
        in_vmem(hour_t),
    )

    anchor_now = anchor_factor
    dest_own = lax.dynamic_slice_in_dim(dest_factor, core * size, size, 1)
    for sweep in range(SWEEPS):
        near, far = sum_dest(message)
        anchor_now, anchor_low, sent = call(
            anchor_kernel,
            [((rank, rows), F32), ((rank, rows), BF16), ((anchor_rows, size), F32)],
            "anchor", half_flops, core_arg, tensor, anchor_now, near, far, hour_gram, hour_t,
        )
        received = swap(sent, "org", 1)
        kept = call(
            anchor_kept_kernel, [((anchor_rows, size), F32)], "anchor_kept", half_flops,
            core_arg, tensor, anchor_low, hour_t, sent,
        )
        near, far = sum_anchor(kept + received)
        dest_own = call(dest_kernel, [((rank, size), F32)], "dest", 0, dest_own, near, far, hour_gram)
        dest_other = swap(dest_own, "org", 1)
        if sweep + 1 < SWEEPS:
            partial = call(
                dest_own_kernel, [((dest_rows, rows), F32)], "dest_own", half_flops,
                core_arg, flipped, dest_own, hour_t,
            )
            message = call(
                dest_other_kernel, [((dest_rows, rows), F32)], "dest_other", half_flops,
                core_arg, flipped, dest_other, hour_t, partial,
            )
    first = jnp.where(core == 0, dest_own, dest_other)
    second = jnp.where(core == 0, dest_other, dest_own)
    return anchor_now, jnp.concatenate([first, second], axis=1)


def solution(mesh):
    return jax.shard_map(
        body,
        mesh=mesh,
        in_specs=(
            P(None, "org", "dst"),
            P(None, "org", "dst"),
            P(None, "org"),
            P(None, "dst"),
            P(),
        ),
        out_specs=(P(None, "org"), P(None, "dst")),
        check_vma=False,
    )
```

```python
import functools

import jax
import jax.numpy as jnp
from jax import lax
from jax.experimental import pallas as pl
from jax.experimental.pallas import tpu as pltpu
from jax.sharding import PartitionSpec as P

SCALE_BLOCK = 128
SWEEPS = 6
F32 = jnp.float32
BF16 = jnp.bfloat16
HIGHEST = lax.Precision.HIGHEST

WHOLE = pl.BlockSpec(memory_space=pltpu.VMEM)
PARAMS = pltpu.CompilerParams(vmem_limit_bytes=8 * 2**20)


def in_vmem(array):
    return pltpu.with_memory_space_constraint(array, pltpu.VMEM)


def gram_rows(rank, width):
    return 8 * -(-(rank // 8) // (width // rank))


def gram_cells(rank, width):
    per_row = width // rank
    for block in range(rank // 8):
        yield block, rank + 8 * (block // per_row), rank * (block % per_row)


def put_gram(message, gram):
    rank = gram.shape[0]
    width = message.shape[1]
    message[rank:, :] = jnp.zeros((message.shape[0] - rank, width), F32)
    for block, row, lane in gram_cells(rank, width):
        message[row : row + 8, lane : lane + rank] = gram[8 * block : 8 * block + 8, :]


def get_gram(message, rank):
    width = message.shape[1]
    return jnp.concatenate(
        [message[row : row + 8, lane : lane + rank] for _, row, lane in gram_cells(rank, width)], axis=0
    )


def own_gram(factor):
    return lax.dot_general(factor, factor, (((1,), (1,)), ((), ())), precision=HIGHEST, preferred_element_type=F32)


def half(flip, size):
    core = lax.axis_index("org") % 2
    start = (1 - core if flip else core) * size
    return pl.ds(pl.multiple_of(start, size), size)


def hour_sum(parts, hour_t):
    total = None
    for hour, part in enumerate(parts):
        term = part * hour_t[:, hour : hour + 1]
        total = term if total is None else total + term
    return total


def first_kernel(
    counts, scales, dest, hour, tensor, message, dest_own, hour_gram, hour_t,
    buffer, scale_now, dest_now, hour_now, arrived, small_arrived,
):
    hours, rows, cols = counts.shape
    small = [
        pltpu.make_async_copy(source, target, small_arrived.at[index])
        for index, (source, target) in enumerate(((scales, scale_now), (dest, dest_now), (hour, hour_now)))
    ]
    for copy in small:
        copy.start()
    large = [pltpu.make_async_copy(counts.at[h], buffer.at[h], arrived.at[h]) for h in range(hours)]
    for copy in large:
        copy.start()
    for copy in small:
        copy.wait()
    hour_t[...] = hour_now[...].T
    hour_gram[...] = own_gram(hour_t[...])
    dest_own[...] = dest_now[:, half(False, cols // 2)]
    dest_low = dest_now[...].astype(BF16)
    put_gram(message, own_gram(dest_now[...]))
    total = None
    for h in range(hours):
        large[h].wait()
        for row_block in range(rows // SCALE_BLOCK):
            row = pl.ds(row_block * SCALE_BLOCK, SCALE_BLOCK)
            for col_block in range(cols // SCALE_BLOCK):
                col = pl.ds(col_block * SCALE_BLOCK, SCALE_BLOCK)
                scale = scale_now[h, row_block, col_block]
                tensor[h, row, col] = (buffer[h, row, col].astype(F32) * scale).astype(BF16)
        part = lax.dot_general(dest_low, tensor[h], (((1,), (1,)), ((), ())), preferred_element_type=F32)
        part = part * hour_t[:, h : h + 1]
        total = part if total is None else total + part
    message[: total.shape[0], :] = total


def flip_kernel(tensor, after, flipped):
    for h in range(tensor.shape[0]):
        flipped[h] = tensor[h].T


def join_kernel(own, other, joined):
    size = own.shape[1]
    joined[:, half(False, size)] = own[...]
    joined[:, half(True, size)] = other[...]


def anchor_kernel(tensor, anchor, near, far, hour_gram, hour_t, _, anchor_out, low_out, sent):
    rank, width = anchor.shape
    message = near[...] + far[...]
    gram_part = get_gram(message, rank) * hour_gram[...]
    low = jnp.dot(gram_part, anchor[...], precision=HIGHEST, preferred_element_type=F32)
    updated = anchor[...] * message[:rank, :] / low
    anchor_out[...] = updated
    anchor_low = updated.astype(BF16)
    low_out[...] = anchor_low
    size = tensor.shape[2] // 2
    cols = half(True, size)
    sent[:rank, :] = hour_sum(
        [jnp.dot(anchor_low, tensor[h, :, cols], preferred_element_type=F32) for h in range(tensor.shape[0])], hour_t
    )
    put_gram(sent, own_gram(updated))


def anchor_kept_kernel(tensor, anchor_low, hour_t, sent, kept):
    rank = anchor_low.shape[0]
    size = tensor.shape[2] // 2
    cols = half(False, size)
    low = anchor_low[...]
    kept[:rank, :] = hour_sum(
        [jnp.dot(low, tensor[h, :, cols], preferred_element_type=F32) for h in range(tensor.shape[0])], hour_t
    )
    kept[rank:, :] = sent[rank:, :]


def dest_kernel(dest, near, far, hour_gram, dest_out):
    rank = dest.shape[0]
    message = near[...] + far[...]
    gram_part = get_gram(message, rank) * hour_gram[...]
    low = jnp.dot(gram_part, dest[...], precision=HIGHEST, preferred_element_type=F32)
    dest_out[...] = dest[...] * message[:rank, :] / low


def dest_own_kernel(flipped, dest, hour_t, message):
    rank = dest.shape[0]
    size = flipped.shape[1] // 2
    rows = half(False, size)
    low = dest[...].astype(BF16)
    message[:rank, :] = hour_sum(
        [jnp.dot(low, flipped[h, rows, :], preferred_element_type=F32) for h in range(flipped.shape[0])], hour_t
    )
    put_gram(message, own_gram(dest[...]))


def dest_other_kernel(flipped, dest, hour_t, before, message):
    rank = dest.shape[0]
    size = flipped.shape[1] // 2
    rows = half(True, size)
    low = dest[...].astype(BF16)
    message[:rank, :] = before[:rank, :] + hour_sum(
        [jnp.dot(low, flipped[h, rows, :], preferred_element_type=F32) for h in range(flipped.shape[0])], hour_t
    )
    put_gram(message, own_gram(dest[...]))
    message[rank:, :] += before[rank:, :]


def call(kernel, outs, name, flops, *args):
    result = pl.pallas_call(
        kernel,
        in_specs=[WHOLE] * len(args),
        out_specs=tuple(WHOLE for _ in outs),
        out_shape=tuple(pltpu.VMEM(shape, dtype) for shape, dtype in outs),
        compiler_params=PARAMS,
        cost_estimate=pl.CostEstimate(flops=flops, bytes_accessed=0, transcendentals=0),
        name=name,
    )(*[in_vmem(arg) for arg in args])
    return result if len(outs) > 1 else result[0]


def swap(array, axis, mask):
    size = lax.axis_size(axis)
    return lax.ppermute(array, axis, [(index, index ^ mask) for index in range(size)])


def sum_dest(message):
    size = lax.axis_size("dst")
    mask = 1
    while 2 * mask < size:
        message = message + swap(message, "dst", 2 * mask - 1)
        mask *= 2
    return message, swap(message, "dst", 2 * mask - 1)


def sum_anchor(message):
    size = lax.axis_size("org")
    if size == 8:
        return message + swap(message, "org", 2), swap(message, "org", 4) + swap(message, "org", 6)
    mask = 2
    while 2 * mask < size:
        message = message + swap(message, "org", mask)
        mask *= 2
    return message, swap(message, "org", mask)


def body(counts, block_scales, anchor_factor, dest_factor, hour_factor):
    hours, rows, cols = counts.shape
    rank = anchor_factor.shape[0]
    size = cols // 2
    dest_rows = rank + gram_rows(rank, rows)
    anchor_rows = rank + gram_rows(rank, size)
    half_flops = 2 * 4 * hours * rank * rows * size

    tensor, message, dest_own, hour_gram, hour_t = pl.pallas_call(
        first_kernel,
        in_specs=[pl.BlockSpec(memory_space=pl.ANY)] * 4,
        out_specs=(WHOLE,) * 5,
        out_shape=(
            pltpu.VMEM((hours, rows, cols), BF16),
            pltpu.VMEM((dest_rows, rows), F32),
            pltpu.VMEM((rank, size), F32),
            pltpu.VMEM((rank, rank), F32),
            pltpu.VMEM((rank, hours), F32),
        ),
        scratch_shapes=[
            pltpu.VMEM(counts.shape, jnp.int32),
            pltpu.SMEM(block_scales.shape, F32),
            pltpu.VMEM(dest_factor.shape, F32),
            pltpu.VMEM(hour_factor.shape, F32),
            pltpu.SemaphoreType.DMA((hours,)),
            pltpu.SemaphoreType.DMA((3,)),
        ],
        compiler_params=pltpu.CompilerParams(vmem_limit_bytes=28 * 2**20),
        name="first",
    )(*[pltpu.with_memory_space_constraint(x, pltpu.HBM) for x in (counts, block_scales, dest_factor, hour_factor)])

    anchor_now = anchor_factor
    for sweep in range(SWEEPS):
        near, far = sum_dest(message)
        if sweep == 0:
            flipped = call(flip_kernel, [((hours, cols, rows), BF16)], "flip", 4 * half_flops, tensor, near)
        anchor_now, anchor_low, sent = call(
            anchor_kernel,
            [((rank, rows), F32), ((rank, rows), BF16), ((anchor_rows, size), F32)],
            "anchor", half_flops, tensor, anchor_now, near, far, hour_gram, hour_t, flipped,
        )
        received = swap(sent, "org", 1)
        kept = call(
            anchor_kept_kernel, [((anchor_rows, size), F32)], "anchor_kept", half_flops,
            tensor, anchor_low, hour_t, sent,
        )
        near, far = sum_anchor(kept + received)
        dest_own = call(dest_kernel, [((rank, size), F32)], "dest", 0, dest_own, near, far, hour_gram)
        dest_other = swap(dest_own, "org", 1)
        if sweep + 1 < SWEEPS:
            partial = call(
                dest_own_kernel, [((dest_rows, rows), F32)], "dest_own", half_flops,
                flipped, dest_own, hour_t,
            )
            message = call(
                dest_other_kernel, [((dest_rows, rows), F32)], "dest_other", half_flops,
                flipped, dest_other, hour_t, partial,
            )
    return anchor_now, call(join_kernel, [((rank, cols), F32)], "join", 0, dest_own, dest_other)


def solution(mesh):
    return jax.shard_map(
        body,
        mesh=mesh,
        in_specs=(
            P(None, "org", "dst"),
            P(None, "org", "dst"),
            P(None, "org"),
            P(None, "dst"),
            P(),
        ),
        out_specs=(P(None, "org"), P(None, "dst")),
        check_vma=False,
    )
```

```python
import functools

import jax
import jax.numpy as jnp
from jax import lax
from jax.experimental import pallas as pl
from jax.experimental.pallas import tpu as pltpu
from jax.sharding import PartitionSpec as P

SCALE_BLOCK = 128
SWEEPS = 6
IN_FLIGHT = 4
F32 = jnp.float32
BF16 = jnp.bfloat16
HIGHEST = lax.Precision.HIGHEST

WHOLE = pl.BlockSpec(memory_space=pltpu.VMEM)
PARAMS = pltpu.CompilerParams(vmem_limit_bytes=8 * 2**20)


def in_vmem(array):
    return pltpu.with_memory_space_constraint(array, pltpu.VMEM)


def gram_rows(rank, width):
    return 8 * -(-(rank // 8) // (width // rank))


def gram_cells(rank, width):
    per_row = width // rank
    for block in range(rank // 8):
        yield block, rank + 8 * (block // per_row), rank * (block % per_row)


def put_gram(message, gram):
    rank = gram.shape[0]
    width = message.shape[1]
    message[rank:, :] = jnp.zeros((message.shape[0] - rank, width), F32)
    for block, row, lane in gram_cells(rank, width):
        message[row : row + 8, lane : lane + rank] = gram[8 * block : 8 * block + 8, :]


def get_gram(message, rank):
    width = message.shape[1]
    return jnp.concatenate(
        [message[row : row + 8, lane : lane + rank] for _, row, lane in gram_cells(rank, width)], axis=0
    )


def own_gram(factor):
    return lax.dot_general(factor, factor, (((1,), (1,)), ((), ())), precision=HIGHEST, preferred_element_type=F32)


def half(flip, size):
    core = lax.axis_index("org") % 2
    start = (1 - core if flip else core) * size
    return pl.ds(pl.multiple_of(start, size), size)


def hour_sum(parts, hour_t):
    total = None
    for hour, part in enumerate(parts):
        term = part * hour_t[:, hour : hour + 1]
        total = term if total is None else total + term
    return total


def first_kernel(
    counts, scales, dest, hour, tensor, message, dest_own, hour_gram, hour_t,
    buffer, scale_now, dest_now, hour_now, arrived, small_arrived,
):
    hours, rows, cols = counts.shape
    small = [
        pltpu.make_async_copy(source, target, small_arrived.at[index])
        for index, (source, target) in enumerate(((scales, scale_now), (dest, dest_now), (hour, hour_now)))
    ]
    for copy in small:
        copy.start()
    large = [pltpu.make_async_copy(counts.at[h], buffer.at[h], arrived.at[h]) for h in range(hours)]
    for copy in large[:IN_FLIGHT]:
        copy.start()
    for copy in small:
        copy.wait()
    hour_t[...] = hour_now[...].T
    hour_gram[...] = own_gram(hour_t[...])
    dest_own[...] = dest_now[:, half(False, cols // 2)]
    dest_low = dest_now[...].astype(BF16)
    put_gram(message, own_gram(dest_now[...]))
    total = None
    for h in range(hours):
        large[h].wait()
        if h + IN_FLIGHT < hours:
            large[h + IN_FLIGHT].start()
        for row_block in range(rows // SCALE_BLOCK):
            row = pl.ds(row_block * SCALE_BLOCK, SCALE_BLOCK)
            scale = jnp.concatenate(
                [
                    jnp.full((1, SCALE_BLOCK), scale_now[h, row_block, col_block], F32)
                    for col_block in range(cols // SCALE_BLOCK)
                ],
                axis=1,
            )
            tensor[h, row, :] = (buffer[h, row, :].astype(F32) * scale).astype(BF16)
        part = lax.dot_general(dest_low, tensor[h], (((1,), (1,)), ((), ())), preferred_element_type=F32)
        part = part * hour_t[:, h : h + 1]
        total = part if total is None else total + part
    message[: total.shape[0], :] = total


def flip_kernel(tensor, after, flipped):
    for h in range(tensor.shape[0]):
        flipped[h] = tensor[h].T


def join_kernel(own, other, joined):
    size = own.shape[1]
    joined[:, half(False, size)] = own[...]
    joined[:, half(True, size)] = other[...]


def anchor_kernel(tensor, anchor, near, far, hour_gram, hour_t, _, anchor_out, low_out, sent):
    rank, width = anchor.shape
    message = near[...] + far[...]
    gram_part = get_gram(message, rank) * hour_gram[...]
    low = jnp.dot(gram_part, anchor[...], precision=HIGHEST, preferred_element_type=F32)
    updated = anchor[...] * message[:rank, :] / low
    anchor_out[...] = updated
    anchor_low = updated.astype(BF16)
    low_out[...] = anchor_low
    size = tensor.shape[2] // 2
    cols = half(True, size)
    sent[:rank, :] = hour_sum(
        [jnp.dot(anchor_low, tensor[h, :, cols], preferred_element_type=F32) for h in range(tensor.shape[0])], hour_t
    )
    put_gram(sent, own_gram(updated))


def anchor_kept_kernel(tensor, anchor_low, hour_t, sent, kept):
    rank = anchor_low.shape[0]
    size = tensor.shape[2] // 2
    cols = half(False, size)
    low = anchor_low[...]
    kept[:rank, :] = hour_sum(
        [jnp.dot(low, tensor[h, :, cols], preferred_element_type=F32) for h in range(tensor.shape[0])], hour_t
    )
    kept[rank:, :] = sent[rank:, :]


def dest_kernel(dest, near, far, hour_gram, dest_out):
    rank = dest.shape[0]
    message = near[...] + far[...]
    gram_part = get_gram(message, rank) * hour_gram[...]
    low = jnp.dot(gram_part, dest[...], precision=HIGHEST, preferred_element_type=F32)
    dest_out[...] = dest[...] * message[:rank, :] / low


def dest_own_kernel(flipped, dest, hour_t, message):
    rank = dest.shape[0]
    size = flipped.shape[1] // 2
    rows = half(False, size)
    low = dest[...].astype(BF16)
    message[:rank, :] = hour_sum(
        [jnp.dot(low, flipped[h, rows, :], preferred_element_type=F32) for h in range(flipped.shape[0])], hour_t
    )
    put_gram(message, own_gram(dest[...]))


def dest_other_kernel(flipped, dest, hour_t, before, message):
    rank = dest.shape[0]
    size = flipped.shape[1] // 2
    rows = half(True, size)
    low = dest[...].astype(BF16)
    message[:rank, :] = before[:rank, :] + hour_sum(
        [jnp.dot(low, flipped[h, rows, :], preferred_element_type=F32) for h in range(flipped.shape[0])], hour_t
    )
    put_gram(message, own_gram(dest[...]))
    message[rank:, :] += before[rank:, :]


def call(kernel, outs, name, flops, *args):
    result = pl.pallas_call(
        kernel,
        in_specs=[WHOLE] * len(args),
        out_specs=tuple(WHOLE for _ in outs),
        out_shape=tuple(pltpu.VMEM(shape, dtype) for shape, dtype in outs),
        compiler_params=PARAMS,
        cost_estimate=pl.CostEstimate(flops=flops, bytes_accessed=0, transcendentals=0),
        name=name,
    )(*[in_vmem(arg) for arg in args])
    return result if len(outs) > 1 else result[0]


def swap(array, axis, mask):
    size = lax.axis_size(axis)
    return lax.ppermute(array, axis, [(index, index ^ mask) for index in range(size)])


def sum_dest(message):
    size = lax.axis_size("dst")
    mask = 1
    while 2 * mask < size:
        message = message + swap(message, "dst", 2 * mask - 1)
        mask *= 2
    return message, swap(message, "dst", 2 * mask - 1)


def sum_anchor(message):
    size = lax.axis_size("org")
    if size == 8:
        return message + swap(message, "org", 2), swap(message, "org", 4) + swap(message, "org", 6)
    mask = 2
    while 2 * mask < size:
        message = message + swap(message, "org", mask)
        mask *= 2
    return message, swap(message, "org", mask)


def body(counts, block_scales, anchor_factor, dest_factor, hour_factor):
    hours, rows, cols = counts.shape
    rank = anchor_factor.shape[0]
    size = cols // 2
    dest_rows = rank + gram_rows(rank, rows)
    anchor_rows = rank + gram_rows(rank, size)
    half_flops = 2 * 4 * hours * rank * rows * size

    tensor, message, dest_own, hour_gram, hour_t = pl.pallas_call(
        first_kernel,
        in_specs=[pl.BlockSpec(memory_space=pl.ANY)] * 4,
        out_specs=(WHOLE,) * 5,
        out_shape=(
            pltpu.VMEM((hours, rows, cols), BF16),
            pltpu.VMEM((dest_rows, rows), F32),
            pltpu.VMEM((rank, size), F32),
            pltpu.VMEM((rank, rank), F32),
            pltpu.VMEM((rank, hours), F32),
        ),
        scratch_shapes=[
            pltpu.VMEM(counts.shape, jnp.int32),
            pltpu.SMEM(block_scales.shape, F32),
            pltpu.VMEM(dest_factor.shape, F32),
            pltpu.VMEM(hour_factor.shape, F32),
            pltpu.SemaphoreType.DMA((hours,)),
            pltpu.SemaphoreType.DMA((3,)),
        ],
        compiler_params=pltpu.CompilerParams(vmem_limit_bytes=28 * 2**20),
        name="first",
    )(*[pltpu.with_memory_space_constraint(x, pltpu.HBM) for x in (counts, block_scales, dest_factor, hour_factor)])

    anchor_now = anchor_factor
    for sweep in range(SWEEPS):
        near, far = sum_dest(message)
        if sweep == 0:
            flipped = call(flip_kernel, [((hours, cols, rows), BF16)], "flip", 4 * half_flops, tensor, near)
        anchor_now, anchor_low, sent = call(
            anchor_kernel,
            [((rank, rows), F32), ((rank, rows), BF16), ((anchor_rows, size), F32)],
            "anchor", half_flops, tensor, anchor_now, near, far, hour_gram, hour_t, flipped,
        )
        received = swap(sent, "org", 1)
        kept = call(
            anchor_kept_kernel, [((anchor_rows, size), F32)], "anchor_kept", half_flops,
            tensor, anchor_low, hour_t, sent,
        )
        near, far = sum_anchor(kept + received)
        dest_own = call(dest_kernel, [((rank, size), F32)], "dest", 0, dest_own, near, far, hour_gram)
        dest_other = swap(dest_own, "org", 1)
        if sweep + 1 < SWEEPS:
            partial = call(
                dest_own_kernel, [((dest_rows, rows), F32)], "dest_own", half_flops,
                flipped, dest_own, hour_t,
            )
            message = call(
                dest_other_kernel, [((dest_rows, rows), F32)], "dest_other", half_flops,
                flipped, dest_other, hour_t, partial,
            )
    return anchor_now, call(join_kernel, [((rank, cols), F32)], "join", 0, dest_own, dest_other)


def solution(mesh):
    return jax.shard_map(
        body,
        mesh=mesh,
        in_specs=(
            P(None, "org", "dst"),
            P(None, "org", "dst"),
            P(None, "org"),
            P(None, "dst"),
            P(),
        ),
        out_specs=(P(None, "org"), P(None, "dst")),
        check_vma=False,
    )
```

```python
import functools

import jax
import jax.numpy as jnp
from jax import lax
from jax.experimental import pallas as pl
from jax.experimental.pallas import tpu as pltpu
from jax.sharding import PartitionSpec as P

SCALE_BLOCK = 128
SWEEPS = 6
IN_FLIGHT = 4
HINT = 10**10
F32 = jnp.float32
BF16 = jnp.bfloat16
HIGHEST = lax.Precision.HIGHEST

WHOLE = pl.BlockSpec(memory_space=pltpu.VMEM)
PARAMS = pltpu.CompilerParams(vmem_limit_bytes=8 * 2**20)


def in_vmem(array):
    return pltpu.with_memory_space_constraint(array, pltpu.VMEM)


def gram_rows(rank, width):
    return 8 * -(-(rank // 8) // (width // rank))


def gram_cells(rank, width):
    per_row = width // rank
    for block in range(rank // 8):
        yield block, rank + 8 * (block // per_row), rank * (block % per_row)


def put_gram(message, gram):
    rank = gram.shape[0]
    width = message.shape[1]
    message[rank:, :] = jnp.zeros((message.shape[0] - rank, width), F32)
    for block, row, lane in gram_cells(rank, width):
        message[row : row + 8, lane : lane + rank] = gram[8 * block : 8 * block + 8, :]


def get_gram(message, rank):
    width = message.shape[1]
    return jnp.concatenate(
        [message[row : row + 8, lane : lane + rank] for _, row, lane in gram_cells(rank, width)], axis=0
    )


def own_gram(factor):
    return lax.dot_general(factor, factor, (((1,), (1,)), ((), ())), precision=HIGHEST, preferred_element_type=F32)


def half(flip, size):
    core = lax.axis_index("org") % 2
    start = (1 - core if flip else core) * size
    return pl.ds(pl.multiple_of(start, size), size)


def hour_sum(parts, hour_t):
    total = None
    for hour, part in enumerate(parts):
        term = part * hour_t[:, hour : hour + 1]
        total = term if total is None else total + term
    return total


def first_kernel(
    counts, scales, dest, hour, tensor, message, message_low, dest_own, hour_gram, hour_t,
    buffer, scale_now, dest_now, hour_now, arrived, small_arrived,
):
    hours, rows, cols = counts.shape
    small = [
        pltpu.make_async_copy(source, target, small_arrived.at[index])
        for index, (source, target) in enumerate(((scales, scale_now), (dest, dest_now), (hour, hour_now)))
    ]
    for copy in small:
        copy.start()
    large = [pltpu.make_async_copy(counts.at[h], buffer.at[h], arrived.at[h]) for h in range(hours)]
    for copy in large[:IN_FLIGHT]:
        copy.start()
    for copy in small:
        copy.wait()
    hour_t[...] = hour_now[...].T
    hour_gram[...] = own_gram(hour_t[...])
    dest_own[...] = dest_now[:, half(False, cols // 2)]
    dest_low = dest_now[...].astype(BF16)
    put_gram(message, own_gram(dest_now[...]))
    total = None
    for h in range(hours):
        large[h].wait()
        if h + IN_FLIGHT < hours:
            large[h + IN_FLIGHT].start()
        for row_block in range(rows // SCALE_BLOCK):
            row = pl.ds(row_block * SCALE_BLOCK, SCALE_BLOCK)
            scale = jnp.concatenate(
                [
                    jnp.full((1, SCALE_BLOCK), scale_now[h, row_block, col_block], F32)
                    for col_block in range(cols // SCALE_BLOCK)
                ],
                axis=1,
            )
            tensor[h, row, :] = (buffer[h, row, :].astype(F32) * scale).astype(BF16)
        part = lax.dot_general(dest_low, tensor[h], (((1,), (1,)), ((), ())), preferred_element_type=F32)
        part = part * hour_t[:, h : h + 1]
        total = part if total is None else total + part
    message[: total.shape[0], :] = total[:, : rows // 2]
    message_low[...] = total[:, rows // 2 :]


def flip_kernel(tensor, after, flipped):
    for h in range(tensor.shape[0]):
        flipped[h] = tensor[h].T


def join_kernel(own, other, upper, lower, joined, stacked):
    size = own.shape[1]
    joined[:, half(False, size)] = own[...]
    joined[:, half(True, size)] = other[...]
    size = upper.shape[1]
    stacked[:, :size] = upper[...]
    stacked[:, size:] = lower[...]


def add_kernel(left, right, *rest):
    total = rest[-1]
    total[...] = left[...] + right[...]


def products(low, tensor, rows, cols, hour_t):
    return hour_sum(
        [jnp.dot(low, tensor[h, rows, cols], preferred_element_type=F32) for h in range(tensor.shape[0])], hour_t
    )


def updated(factor, totals, gram_part):
    return factor * totals / jnp.dot(gram_part, factor, precision=HIGHEST, preferred_element_type=F32)


def upper_kernel(tensor, anchor, near, far, hour_gram, hour_t, anchor_out, gram_part, gram, sent, kept):
    rank, width = anchor.shape
    message = near[...] + far[...]
    gram_part[...] = get_gram(message, rank) * hour_gram[...]
    anchor_out[...] = updated(anchor[...], message[:rank, :], gram_part[...])
    low = anchor_out[...].astype(BF16)
    size = tensor.shape[2] // 2
    sent[...] = products(low, tensor, pl.ds(0, width), half(True, size), hour_t)
    kept[...] = products(low, tensor, pl.ds(0, width), half(False, size), hour_t)
    gram[...] = own_gram(anchor_out[...])


def lower_kernel(tensor, anchor, near, far, gram_part, hour_t, gram, before, _, anchor_out, sent):
    rank, width = anchor.shape
    anchor_out[...] = updated(anchor[...], near[...] + far[...], gram_part[...])
    low = anchor_out[...].astype(BF16)
    size = tensor.shape[2] // 2
    sent[:rank, :] = before[...] + products(low, tensor, pl.ds(width, width), half(True, size), hour_t)
    put_gram(sent, gram[...] + own_gram(anchor_out[...]))


def lower_kept_kernel(tensor, anchor, hour_t, before, sent, kept):
    rank, width = anchor.shape
    low = anchor[...].astype(BF16)
    size = tensor.shape[2] // 2
    kept[:rank, :] = before[...] + products(low, tensor, pl.ds(width, width), half(False, size), hour_t)
    kept[rank:, :] = sent[rank:, :]


def dest_kernel(dest, near, far, hour_gram, dest_out):
    rank = dest.shape[0]
    message = near[...] + far[...]
    gram_part = get_gram(message, rank) * hour_gram[...]
    dest_out[...] = updated(dest[...], message[:rank, :], gram_part)


def dest_own_kernel(flipped, dest, hour_t, upper, lower, gram):
    low = dest[...].astype(BF16)
    rows = half(False, flipped.shape[1] // 2)
    width = flipped.shape[2] // 2
    upper[...] = products(low, flipped, rows, pl.ds(0, width), hour_t)
    lower[...] = products(low, flipped, rows, pl.ds(width, width), hour_t)
    gram[...] = own_gram(dest[...])


def dest_upper_kernel(flipped, dest, hour_t, before, gram, message):
    low = dest[...].astype(BF16)
    rows = half(True, flipped.shape[1] // 2)
    width = flipped.shape[2] // 2
    message[: low.shape[0], :] = before[...] + products(low, flipped, rows, pl.ds(0, width), hour_t)
    put_gram(message, gram[...] + own_gram(dest[...]))


def dest_lower_kernel(flipped, dest, hour_t, before, message):
    low = dest[...].astype(BF16)
    rows = half(True, flipped.shape[1] // 2)
    width = flipped.shape[2] // 2
    message[...] = before[...] + products(low, flipped, rows, pl.ds(width, width), hour_t)


def call(kernel, outs, name, flops, *args):
    result = pl.pallas_call(
        kernel,
        in_specs=[WHOLE] * len(args),
        out_specs=tuple(WHOLE for _ in outs),
        out_shape=tuple(pltpu.VMEM(shape, dtype) for shape, dtype in outs),
        compiler_params=PARAMS,
        cost_estimate=pl.CostEstimate(flops=flops, bytes_accessed=0, transcendentals=0),
        name=name,
    )(*[in_vmem(arg) for arg in args])
    return result if len(outs) > 1 else result[0]


def swap(array, axis, mask):
    size = lax.axis_size(axis)
    return lax.ppermute(array, axis, [(index, index ^ mask) for index in range(size)])


def sum_dest(message, *before):
    size = lax.axis_size("dst")
    mask = 1
    while 2 * mask < size:
        message = call(add_kernel, [(message.shape, F32)], "add", HINT, message, swap(message, "dst", mask), *before)
        mask *= 2
    return message, swap(message, "dst", mask)


def sum_anchor(message):
    size = lax.axis_size("org")
    if size == 8:
        return message + swap(message, "org", 2), swap(message, "org", 4) + swap(message, "org", 6)
    mask = 2
    while 2 * mask < size:
        message = message + swap(message, "org", mask)
        mask *= 2
    return message, swap(message, "org", mask)


def body(counts, block_scales, anchor_factor, dest_factor, hour_factor):
    hours, rows, cols = counts.shape
    rank = anchor_factor.shape[0]
    size = cols // 2
    width = rows // 2
    dest_rows = rank + gram_rows(rank, width)
    anchor_rows = rank + gram_rows(rank, size)
    half_flops = 2 * 4 * hours * rank * rows * size

    tensor, message, message_low, dest_own, hour_gram, hour_t = pl.pallas_call(
        first_kernel,
        in_specs=[pl.BlockSpec(memory_space=pl.ANY)] * 4,
        out_specs=(WHOLE,) * 6,
        out_shape=(
            pltpu.VMEM((hours, rows, cols), BF16),
            pltpu.VMEM((dest_rows, width), F32),
            pltpu.VMEM((rank, width), F32),
            pltpu.VMEM((rank, size), F32),
            pltpu.VMEM((rank, rank), F32),
            pltpu.VMEM((rank, hours), F32),
        ),
        scratch_shapes=[
            pltpu.VMEM(counts.shape, jnp.int32),
            pltpu.SMEM(block_scales.shape, F32),
            pltpu.VMEM(dest_factor.shape, F32),
            pltpu.VMEM(hour_factor.shape, F32),
            pltpu.SemaphoreType.DMA((hours,)),
            pltpu.SemaphoreType.DMA((3,)),
        ],
        compiler_params=pltpu.CompilerParams(vmem_limit_bytes=28 * 2**20),
        name="first",
    )(*[pltpu.with_memory_space_constraint(x, pltpu.HBM) for x in (counts, block_scales, dest_factor, hour_factor)])

    upper, lower = anchor_factor[:, :width], anchor_factor[:, width:]
    for sweep in range(SWEEPS):
        near, far = sum_dest(message)
        near_low, far_low = sum_dest(message_low)
        if sweep == 0:
            flipped = call(flip_kernel, [((hours, cols, rows), BF16)], "flip", 4 * half_flops, tensor, near)
        upper, gram_part, gram, sent, kept = call(
            upper_kernel,
            [((rank, width), F32), ((rank, rank), F32), ((rank, rank), F32), ((rank, size), F32), ((rank, size), F32)],
            "upper", half_flops, tensor, upper, near, far, hour_gram, hour_t,
        )
        lower, sent = call(
            lower_kernel, [((rank, width), F32), ((anchor_rows, size), F32)], "lower", half_flops // 2,
            tensor, lower, near_low, far_low, gram_part, hour_t, gram, sent, flipped,
        )
        received = swap(sent, "org", 1)
        kept = call(
            lower_kept_kernel, [((anchor_rows, size), F32)], "lower_kept", half_flops // 2,
            tensor, lower, hour_t, kept, sent,
        )
        near, far = sum_anchor(kept + received)
        dest_own = call(dest_kernel, [((rank, size), F32)], "dest", 0, dest_own, near, far, hour_gram)
        dest_other = swap(dest_own, "org", 1)
        if sweep + 1 < SWEEPS:
            part, part_low, gram = call(
                dest_own_kernel, [((rank, width), F32), ((rank, width), F32), ((rank, rank), F32)], "dest_own",
                half_flops, flipped, dest_own, hour_t,
            )
            message = call(
                dest_upper_kernel, [((dest_rows, width), F32)], "dest_upper", half_flops // 2,
                flipped, dest_other, hour_t, part, gram,
            )
            message_low = call(
                dest_lower_kernel, [((rank, width), F32)], "dest_lower", half_flops // 2,
                flipped, dest_other, hour_t, part_low,
            )
    dest_now, anchor_now = call(
        join_kernel, [((rank, cols), F32), ((rank, rows), F32)], "join", 0, dest_own, dest_other, upper, lower
    )
    return anchor_now, dest_now


def solution(mesh):
    return jax.shard_map(
        body,
        mesh=mesh,
        in_specs=(
            P(None, "org", "dst"),
            P(None, "org", "dst"),
            P(None, "org"),
            P(None, "dst"),
            P(),
        ),
        out_specs=(P(None, "org"), P(None, "dst")),
        check_vma=False,
    )
```

```python
import functools

import jax
import jax.numpy as jnp
from jax import lax
from jax.experimental import pallas as pl
from jax.experimental.pallas import tpu as pltpu
from jax.sharding import PartitionSpec as P

SCALE_BLOCK = 128
SWEEPS = 6
IN_FLIGHT = 4
HINT = 10**10
F32 = jnp.float32
BF16 = jnp.bfloat16

WHOLE = pl.BlockSpec(memory_space=pltpu.VMEM)
ANYWHERE = pl.BlockSpec(memory_space=pl.ANY)
PARAMS = pltpu.CompilerParams(vmem_limit_bytes=8 * 2**20)


def in_vmem(array):
    return pltpu.with_memory_space_constraint(array, pltpu.VMEM)


def gram_rows(rank, width):
    return 8 * -(-(rank // 8) // (width // rank))


def gram_cells(rank, width):
    per_row = width // rank
    for block in range(rank // 8):
        yield block, rank + 8 * (block // per_row), rank * (block % per_row)


def put_gram(message, gram):
    rank = gram.shape[0]
    width = message.shape[1]
    message[rank:, :] = jnp.zeros((message.shape[0] - rank, width), F32)
    for block, row, lane in gram_cells(rank, width):
        message[row : row + 8, lane : lane + rank] = gram[8 * block : 8 * block + 8, :]


def get_gram(message, rank):
    width = message.shape[1]
    return jnp.concatenate(
        [message[row : row + 8, lane : lane + rank] for _, row, lane in gram_cells(rank, width)], axis=0
    )


def parts_of(array):
    high = array.astype(BF16)
    return high, (array - high.astype(F32)).astype(BF16)


def own_gram(factor):
    def dot(left, right):
        return lax.dot_general(left, right, (((1,), (1,)), ((), ())), preferred_element_type=F32)

    high, low = parts_of(factor)
    return dot(high, high) + (dot(high, low) + dot(low, high))


def times(left, right):
    left_high, left_low = parts_of(left)
    right_high, right_low = parts_of(right)
    return jnp.dot(
        jnp.concatenate([left_high, left_low, left_high], axis=1),
        jnp.concatenate([right_high, right_high, right_low], axis=0),
        preferred_element_type=F32,
    )


def half(flip, size):
    core = lax.axis_index("org") % 2
    start = (1 - core if flip else core) * size
    return pl.ds(pl.multiple_of(start, size), size)


def hour_sum(parts, hour_t):
    total = None
    for hour, part in enumerate(parts):
        term = part * hour_t[:, hour : hour + 1]
        total = term if total is None else total + term
    return total


def first_kernel(
    counts, scales, dest, hour, tensor, message, message_low, dest_own, hour_gram, hour_t,
    buffer, scale_now, dest_now, hour_now, arrived, small_arrived,
):
    hours, rows, cols = counts.shape
    small = [
        pltpu.make_async_copy(source, target, small_arrived.at[index])
        for index, (source, target) in enumerate(((scales, scale_now), (dest, dest_now), (hour, hour_now)))
    ]
    for copy in small:
        copy.start()
    large = [pltpu.make_async_copy(counts.at[h], buffer.at[h], arrived.at[h]) for h in range(hours)]
    for copy in large[:IN_FLIGHT]:
        copy.start()
    for copy in small:
        copy.wait()
    hour_t[...] = hour_now[...].T
    hour_gram[...] = own_gram(hour_t[...])
    dest_own[...] = dest_now[:, half(False, cols // 2)]
    dest_low = dest_now[...].astype(BF16)
    put_gram(message, own_gram(dest_now[...]))
    total = None
    for h in range(hours):
        large[h].wait()
        if h + IN_FLIGHT < hours:
            large[h + IN_FLIGHT].start()
        for row_block in range(rows // SCALE_BLOCK):
            row = pl.ds(row_block * SCALE_BLOCK, SCALE_BLOCK)
            scale = jnp.concatenate(
                [
                    jnp.full((1, SCALE_BLOCK), scale_now[h, row_block, col_block], F32)
                    for col_block in range(cols // SCALE_BLOCK)
                ],
                axis=1,
            )
            tensor[h, row, :] = (buffer[h, row, :].astype(F32) * scale).astype(BF16)
        part = lax.dot_general(dest_low, tensor[h], (((1,), (1,)), ((), ())), preferred_element_type=F32)
        part = part * hour_t[:, h : h + 1]
        total = part if total is None else total + part
    message[: total.shape[0], :] = total[:, : rows // 2]
    message_low[...] = total[:, rows // 2 :]


def flip_kernel(tensor, after, flipped):
    for h in range(tensor.shape[0]):
        flipped[h] = tensor[h].T


def store(copies, done):
    started = [
        pltpu.make_async_copy(source, target, done.at[index]) for index, (source, target) in enumerate(copies)
    ]
    for copy in started:
        copy.start()
    for copy in started:
        copy.wait()


def store_own_kernel(upper, lower, own, anchor_out, dest_out, done):
    width = upper.shape[1]
    store(
        (
            (upper, anchor_out.at[:, pl.ds(0, width)]),
            (lower, anchor_out.at[:, pl.ds(width, width)]),
            (own, dest_out.at[:, half(False, own.shape[1])]),
        ),
        done,
    )


def store_other_kernel(other, _, dest_out, done):
    store(((other, dest_out.at[:, half(True, other.shape[1])]),), done)


def add_kernel(left, right, *rest):
    total = rest[-1]
    total[...] = left[...] + right[...]


def products(low, tensor, rows, cols, hour_t):
    return hour_sum(
        [jnp.dot(low, tensor[h, rows, cols], preferred_element_type=F32) for h in range(tensor.shape[0])], hour_t
    )


def updated(factor, totals, gram_part):
    return factor * totals / times(gram_part, factor)


def upper_kernel(tensor, anchor, near, far, hour_gram, hour_t, anchor_out, gram_part, gram, sent, kept):
    rank, width = anchor.shape
    message = near[...] + far[...]
    gram_part[...] = get_gram(message, rank) * hour_gram[...]
    anchor_out[...] = updated(anchor[...], message[:rank, :], gram_part[...])
    low = anchor_out[...].astype(BF16)
    size = tensor.shape[2] // 2
    sent[...] = products(low, tensor, pl.ds(0, width), half(True, size), hour_t)
    kept[...] = products(low, tensor, pl.ds(0, width), half(False, size), hour_t)
    gram[...] = own_gram(anchor_out[...])


def lower_kernel(tensor, anchor, near, far, gram_part, hour_t, gram, before, _, anchor_out, sent):
    rank, width = anchor.shape
    anchor_out[...] = updated(anchor[...], near[...] + far[...], gram_part[...])
    low = anchor_out[...].astype(BF16)
    size = tensor.shape[2] // 2
    sent[:rank, :] = before[...] + products(low, tensor, pl.ds(width, width), half(True, size), hour_t)
    put_gram(sent, gram[...] + own_gram(anchor_out[...]))


def lower_kept_kernel(tensor, anchor, hour_t, before, sent, kept):
    rank, width = anchor.shape
    low = anchor[...].astype(BF16)
    size = tensor.shape[2] // 2
    kept[:rank, :] = before[...] + products(low, tensor, pl.ds(width, width), half(False, size), hour_t)
    kept[rank:, :] = sent[rank:, :]


def dest_kernel(dest, near, far, hour_gram, dest_out):
    rank = dest.shape[0]
    message = near[...] + far[...]
    gram_part = get_gram(message, rank) * hour_gram[...]
    dest_out[...] = updated(dest[...], message[:rank, :], gram_part)


def dest_own_kernel(flipped, dest, hour_t, upper, lower, gram):
    low = dest[...].astype(BF16)
    rows = half(False, flipped.shape[1] // 2)
    width = flipped.shape[2] // 2
    upper[...] = products(low, flipped, rows, pl.ds(0, width), hour_t)
    lower[...] = products(low, flipped, rows, pl.ds(width, width), hour_t)
    gram[...] = own_gram(dest[...])


def dest_upper_kernel(flipped, dest, hour_t, before, gram, message):
    low = dest[...].astype(BF16)
    rows = half(True, flipped.shape[1] // 2)
    width = flipped.shape[2] // 2
    message[: low.shape[0], :] = before[...] + products(low, flipped, rows, pl.ds(0, width), hour_t)
    put_gram(message, gram[...] + own_gram(dest[...]))


def dest_lower_kernel(flipped, dest, hour_t, before, message):
    low = dest[...].astype(BF16)
    rows = half(True, flipped.shape[1] // 2)
    width = flipped.shape[2] // 2
    message[...] = before[...] + products(low, flipped, rows, pl.ds(width, width), hour_t)


def call(kernel, outs, name, flops, *args):
    result = pl.pallas_call(
        kernel,
        in_specs=[WHOLE] * len(args),
        out_specs=tuple(WHOLE for _ in outs),
        out_shape=tuple(pltpu.VMEM(shape, dtype) for shape, dtype in outs),
        compiler_params=PARAMS,
        cost_estimate=pl.CostEstimate(flops=flops, bytes_accessed=0, transcendentals=0),
        name=name,
    )(*[in_vmem(arg) for arg in args])
    return result if len(outs) > 1 else result[0]


def swap(array, axis, mask):
    size = lax.axis_size(axis)
    return lax.ppermute(array, axis, [(index, index ^ mask) for index in range(size)])


def sum_dest(message, *before):
    size = lax.axis_size("dst")
    mask = 1
    while 2 * mask < size:
        message = call(add_kernel, [(message.shape, F32)], "add", HINT, message, swap(message, "dst", mask), *before)
        mask *= 2
    return message, swap(message, "dst", mask)


def sum_anchor(message):
    size = lax.axis_size("org")
    if size == 8:
        return message + swap(message, "org", 2), swap(message, "org", 4) + swap(message, "org", 6)
    mask = 2
    while 2 * mask < size:
        message = message + swap(message, "org", mask)
        mask *= 2
    return message, swap(message, "org", mask)


def body(counts, block_scales, anchor_factor, dest_factor, hour_factor):
    hours, rows, cols = counts.shape
    rank = anchor_factor.shape[0]
    size = cols // 2
    width = rows // 2
    dest_rows = rank + gram_rows(rank, width)
    anchor_rows = rank + gram_rows(rank, size)
    half_flops = 2 * 4 * hours * rank * rows * size

    tensor, message, message_low, dest_own, hour_gram, hour_t = pl.pallas_call(
        first_kernel,
        in_specs=[ANYWHERE] * 4,
        out_specs=(WHOLE,) * 6,
        out_shape=(
            pltpu.VMEM((hours, rows, cols), BF16),
            pltpu.VMEM((dest_rows, width), F32),
            pltpu.VMEM((rank, width), F32),
            pltpu.VMEM((rank, size), F32),
            pltpu.VMEM((rank, rank), F32),
            pltpu.VMEM((rank, hours), F32),
        ),
        scratch_shapes=[
            pltpu.VMEM(counts.shape, jnp.int32),
            pltpu.SMEM(block_scales.shape, F32),
            pltpu.VMEM(dest_factor.shape, F32),
            pltpu.VMEM(hour_factor.shape, F32),
            pltpu.SemaphoreType.DMA((hours,)),
            pltpu.SemaphoreType.DMA((3,)),
        ],
        compiler_params=pltpu.CompilerParams(vmem_limit_bytes=28 * 2**20),
        name="first",
    )(*[pltpu.with_memory_space_constraint(x, pltpu.HBM) for x in (counts, block_scales, dest_factor, hour_factor)])

    upper, lower = anchor_factor[:, :width], anchor_factor[:, width:]
    for sweep in range(SWEEPS):
        near, far = sum_dest(message)
        near_low, far_low = sum_dest(message_low)
        if sweep == 0:
            flipped = call(flip_kernel, [((hours, cols, rows), BF16)], "flip", 4 * half_flops, tensor, near)
        upper, gram_part, gram, sent, kept = call(
            upper_kernel,
            [((rank, width), F32), ((rank, rank), F32), ((rank, rank), F32), ((rank, size), F32), ((rank, size), F32)],
            "upper", half_flops, tensor, upper, near, far, hour_gram, hour_t,
        )
        lower, sent = call(
            lower_kernel, [((rank, width), F32), ((anchor_rows, size), F32)], "lower", half_flops // 2,
            tensor, lower, near_low, far_low, gram_part, hour_t, gram, sent, flipped,
        )
        received = swap(sent, "org", 1)
        kept = call(
            lower_kept_kernel, [((anchor_rows, size), F32)], "lower_kept", half_flops // 2,
            tensor, lower, hour_t, kept, sent,
        )
        near, far = sum_anchor(kept + received)
        dest_own = call(dest_kernel, [((rank, size), F32)], "dest", 0, dest_own, near, far, hour_gram)
        dest_other = swap(dest_own, "org", 1)
        if sweep + 1 < SWEEPS:
            part, part_low, gram = call(
                dest_own_kernel, [((rank, width), F32), ((rank, width), F32), ((rank, rank), F32)], "dest_own",
                half_flops, flipped, dest_own, hour_t,
            )
            message = call(
                dest_upper_kernel, [((dest_rows, width), F32)], "dest_upper", half_flops // 2,
                flipped, dest_other, hour_t, part, gram,
            )
            message_low = call(
                dest_lower_kernel, [((rank, width), F32)], "dest_lower", half_flops // 2,
                flipped, dest_other, hour_t, part_low,
            )
    anchor_now, dest_now = pl.pallas_call(
        store_own_kernel,
        in_specs=[WHOLE] * 3,
        out_specs=(ANYWHERE,) * 2,
        out_shape=(pltpu.HBM((rank, rows), F32), pltpu.HBM((rank, cols), F32)),
        scratch_shapes=[pltpu.SemaphoreType.DMA((3,))],
        compiler_params=PARAMS,
        name="store_own",
    )(in_vmem(upper), in_vmem(lower), in_vmem(dest_own))
    dest_now = pl.pallas_call(
        store_other_kernel,
        in_specs=[WHOLE, ANYWHERE],
        out_specs=ANYWHERE,
        out_shape=pltpu.HBM((rank, cols), F32),
        scratch_shapes=[pltpu.SemaphoreType.DMA((1,))],
        input_output_aliases={1: 0},
        compiler_params=PARAMS,
        name="store_other",
    )(in_vmem(dest_other), pltpu.with_memory_space_constraint(dest_now, pltpu.HBM))
    return anchor_now, dest_now


def solution(mesh):
    return jax.shard_map(
        body,
        mesh=mesh,
        in_specs=(
            P(None, "org", "dst"),
            P(None, "org", "dst"),
            P(None, "org"),
            P(None, "dst"),
            P(),
        ),
        out_specs=(P(None, "org"), P(None, "dst")),
        check_vma=False,
    )
```

```python
import functools

import jax
import jax.numpy as jnp
from jax import lax
from jax.experimental import pallas as pl
from jax.experimental.pallas import tpu as pltpu
from jax.sharding import PartitionSpec as P

SCALE_BLOCK = 128
SWEEPS = 6
IN_FLIGHT = 4
HINT = 10**10
F32 = jnp.float32
BF16 = jnp.bfloat16

WHOLE = pl.BlockSpec(memory_space=pltpu.VMEM)
ANYWHERE = pl.BlockSpec(memory_space=pl.ANY)
PARAMS = pltpu.CompilerParams(vmem_limit_bytes=8 * 2**20)


def in_vmem(array):
    return pltpu.with_memory_space_constraint(array, pltpu.VMEM)


def gram_rows(rank, width):
    return 8 * -(-(rank // 8) // (width // rank))


def gram_cells(rank, width):
    per_row = width // rank
    for block in range(rank // 8):
        yield block, rank + 8 * (block // per_row), rank * (block % per_row)


def put_gram(message, gram):
    rank = gram.shape[0]
    width = message.shape[1]
    message[rank:, :] = jnp.zeros((message.shape[0] - rank, width), F32)
    for block, row, lane in gram_cells(rank, width):
        message[row : row + 8, lane : lane + rank] = gram[8 * block : 8 * block + 8, :]


def get_gram(message, rank):
    width = message.shape[1]
    return jnp.concatenate(
        [message[row : row + 8, lane : lane + rank] for _, row, lane in gram_cells(rank, width)], axis=0
    )


def parts_of(array):
    high = array.astype(BF16)
    return high, (array - high.astype(F32)).astype(BF16)


def own_gram(factor):
    def dot(left, right):
        return lax.dot_general(left, right, (((1,), (1,)), ((), ())), preferred_element_type=F32)

    high, low = parts_of(factor)
    return dot(high, high) + (dot(high, low) + dot(low, high))


def times(left, right):
    left_high, left_low = parts_of(left)
    right_high, right_low = parts_of(right)
    return jnp.dot(
        jnp.concatenate([left_high, left_low, left_high], axis=1),
        jnp.concatenate([right_high, right_high, right_low], axis=0),
        preferred_element_type=F32,
    )


def half(flip, size, part=None):
    core = lax.axis_index("org") % 2
    start = (1 - core if flip else core) * size
    if part is None:
        return pl.ds(pl.multiple_of(start, size), size)
    size //= 2
    return pl.ds(pl.multiple_of(start + part * size, size), size)


def hour_sum(parts, hour_t):
    total = None
    for hour, part in enumerate(parts):
        term = part * hour_t[:, hour : hour + 1]
        total = term if total is None else total + term
    return total


def first_kernel(
    counts, scales, dest, hour, tensor, message, message_low, dest_own, dest_late, hour_gram, hour_t,
    buffer, scale_now, dest_now, hour_now, arrived, small_arrived,
):
    hours, rows, cols = counts.shape
    small = [
        pltpu.make_async_copy(source, target, small_arrived.at[index])
        for index, (source, target) in enumerate(((scales, scale_now), (dest, dest_now), (hour, hour_now)))
    ]
    for copy in small:
        copy.start()
    large = [pltpu.make_async_copy(counts.at[h], buffer.at[h], arrived.at[h]) for h in range(hours)]
    for copy in large[:IN_FLIGHT]:
        copy.start()
    for copy in small:
        copy.wait()
    hour_t[...] = hour_now[...].T
    hour_gram[...] = own_gram(hour_t[...])
    dest_own[...] = dest_now[:, half(False, cols // 2, 0)]
    dest_late[...] = dest_now[:, half(False, cols // 2, 1)]
    dest_low = dest_now[...].astype(BF16)
    put_gram(message, own_gram(dest_now[...]))
    total = None
    for h in range(hours):
        large[h].wait()
        if h + IN_FLIGHT < hours:
            large[h + IN_FLIGHT].start()
        for row_block in range(rows // SCALE_BLOCK):
            row = pl.ds(row_block * SCALE_BLOCK, SCALE_BLOCK)
            scale = jnp.concatenate(
                [
                    jnp.full((1, SCALE_BLOCK), scale_now[h, row_block, col_block], F32)
                    for col_block in range(cols // SCALE_BLOCK)
                ],
                axis=1,
            )
            tensor[h, row, :] = (buffer[h, row, :].astype(F32) * scale).astype(BF16)
        part = lax.dot_general(dest_low, tensor[h], (((1,), (1,)), ((), ())), preferred_element_type=F32)
        part = part * hour_t[:, h : h + 1]
        total = part if total is None else total + part
    message[: total.shape[0], :] = total[:, : rows // 2]
    message_low[...] = total[:, rows // 2 :]


def flip_kernel(tensor, after, flipped):
    for h in range(tensor.shape[0]):
        flipped[h] = tensor[h].T


def store(copies, done):
    started = [
        pltpu.make_async_copy(source, target, done.at[index]) for index, (source, target) in enumerate(copies)
    ]
    for copy in started:
        copy.start()
    for copy in started:
        copy.wait()


def store_own_kernel(upper, lower, own, late, anchor_out, dest_out, done):
    width = upper.shape[1]
    size = 2 * own.shape[1]
    store(
        (
            (upper, anchor_out.at[:, pl.ds(0, width)]),
            (lower, anchor_out.at[:, pl.ds(width, width)]),
            (own, dest_out.at[:, half(False, size, 0)]),
            (late, dest_out.at[:, half(False, size, 1)]),
        ),
        done,
    )


def store_other_kernel(other, late, _, dest_out, done):
    size = 2 * other.shape[1]
    store(((other, dest_out.at[:, half(True, size, 0)]), (late, dest_out.at[:, half(True, size, 1)])), done)


def add_kernel(left, right, total):
    total[...] = left[...] + right[...]


def products(low, tensor, rows, cols, hour_t):
    return hour_sum(
        [jnp.dot(low, tensor[h, rows, cols], preferred_element_type=F32) for h in range(tensor.shape[0])], hour_t
    )


def updated(factor, totals, gram_part):
    return factor * totals / times(gram_part, factor)


def upper_kernel(tensor, anchor, near, far, hour_gram, hour_t, anchor_out, gram_part, gram, sent, kept):
    rank, width = anchor.shape
    message = near[...] + far[...]
    gram_part[...] = get_gram(message, rank) * hour_gram[...]
    anchor_out[...] = updated(anchor[...], message[:rank, :], gram_part[...])
    low = anchor_out[...].astype(BF16)
    size = tensor.shape[2] // 2
    sent[...] = products(low, tensor, pl.ds(0, width), half(True, size), hour_t)
    kept[...] = products(low, tensor, pl.ds(0, width), half(False, size), hour_t)
    gram[...] = own_gram(anchor_out[...])


def lower_kernel(tensor, anchor, near, far, gram_part, hour_t, before, _, anchor_out, sent):
    width = anchor.shape[1]
    anchor_out[...] = updated(anchor[...], near[...] + far[...], gram_part[...])
    low = anchor_out[...].astype(BF16)
    cols = half(True, tensor.shape[2] // 2, 0)
    sent[...] = before[:, : cols.size] + products(low, tensor, pl.ds(width, width), cols, hour_t)


def lower_late_kernel(tensor, anchor, hour_t, gram, before, sent):
    rank, width = anchor.shape
    low = anchor[...].astype(BF16)
    cols = half(True, tensor.shape[2] // 2, 1)
    sent[:rank, :] = before[:, cols.size :] + products(low, tensor, pl.ds(width, width), cols, hour_t)
    put_gram(sent, gram[...] + own_gram(anchor[...]))


def lower_kept_kernel(tensor, anchor, hour_t, before, sent, kept, kept_late):
    rank, width = anchor.shape
    low = anchor[...].astype(BF16)
    size = tensor.shape[2] // 2
    total = before[...] + products(low, tensor, pl.ds(width, width), half(False, size), hour_t)
    kept[...] = total[:, : size // 2]
    kept_late[:rank, :] = total[:, size // 2 :]
    kept_late[rank:, :] = sent[rank:, :]


def dest_late_kernel(dest, near, far, hour_gram, dest_out, gram_part):
    rank = dest.shape[0]
    message = near[...] + far[...]
    gram_part[...] = get_gram(message, rank) * hour_gram[...]
    dest_out[...] = updated(dest[...], message[:rank, :], gram_part[...])


def dest_kernel(dest, near, far, gram_part, dest_out):
    dest_out[...] = updated(dest[...], near[...] + far[...], gram_part[...])


def dest_products(dest, flipped, flip, part, width, index, hour_t):
    rows = half(flip, flipped.shape[1] // 2, part)
    return products(dest[...].astype(BF16), flipped, rows, pl.ds(index * width, width), hour_t)


def own_late_kernel(flipped, dest, hour_t, upper, lower, gram):
    width = upper.shape[1]
    upper[...] = dest_products(dest, flipped, False, 1, width, 0, hour_t)
    lower[...] = dest_products(dest, flipped, False, 1, width, 1, hour_t)
    gram[...] = own_gram(dest[...])


def more_kernel(flip, part, flipped, dest, hour_t, upper, lower, gram, upper_out, lower_out, gram_out):
    width = upper.shape[1]
    upper_out[...] = upper[...] + dest_products(dest, flipped, flip, part, width, 0, hour_t)
    lower_out[...] = lower[...] + dest_products(dest, flipped, flip, part, width, 1, hour_t)
    gram_out[...] = gram[...] + own_gram(dest[...])


def dest_upper_kernel(flipped, dest, hour_t, before, gram, message):
    rank, width = before.shape
    message[:rank, :] = before[...] + dest_products(dest, flipped, True, 0, width, 0, hour_t)
    put_gram(message, gram[...] + own_gram(dest[...]))


def dest_lower_kernel(flipped, dest, hour_t, before, message):
    message[...] = before[...] + dest_products(dest, flipped, True, 0, before.shape[1], 1, hour_t)


def call(kernel, outs, name, flops, *args):
    result = pl.pallas_call(
        kernel,
        in_specs=[WHOLE] * len(args),
        out_specs=tuple(WHOLE for _ in outs),
        out_shape=tuple(pltpu.VMEM(shape, dtype) for shape, dtype in outs),
        compiler_params=PARAMS,
        cost_estimate=pl.CostEstimate(flops=flops, bytes_accessed=0, transcendentals=0),
        name=name,
    )(*[in_vmem(arg) for arg in args])
    return result if len(outs) > 1 else result[0]


def swap(array, axis, mask):
    size = lax.axis_size(axis)
    return lax.ppermute(array, axis, [(index, index ^ mask) for index in range(size)])


def add(left, right):
    return call(add_kernel, [(left.shape, F32)], "add", HINT, left, right)


def sum_steps(message, axis, mask):
    size = lax.axis_size(axis)
    while 2 * mask < size:
        message = add(message, swap(message, axis, mask))
        mask *= 2
    return message, swap(message, axis, mask)


def sum_at_once(message):
    if lax.axis_size("org") != 8:
        return sum_steps(message, "org", 2)
    return message + swap(message, "org", 2), swap(message, "org", 4) + swap(message, "org", 6)


def body(counts, block_scales, anchor_factor, dest_factor, hour_factor):
    hours, rows, cols = counts.shape
    rank = anchor_factor.shape[0]
    size = cols // 2
    width = rows // 2
    dest_rows = rank + gram_rows(rank, width)
    part_size = size // 2
    anchor_rows = rank + gram_rows(rank, part_size)
    half_flops = 2 * 4 * hours * rank * rows * size

    tensor, message, message_low, dest_own, late_own, hour_gram, hour_t = pl.pallas_call(
        first_kernel,
        in_specs=[ANYWHERE] * 4,
        out_specs=(WHOLE,) * 7,
        out_shape=(
            pltpu.VMEM((hours, rows, cols), BF16),
            pltpu.VMEM((dest_rows, width), F32),
            pltpu.VMEM((rank, width), F32),
            pltpu.VMEM((rank, part_size), F32),
            pltpu.VMEM((rank, part_size), F32),
            pltpu.VMEM((rank, rank), F32),
            pltpu.VMEM((rank, hours), F32),
        ),
        scratch_shapes=[
            pltpu.VMEM(counts.shape, jnp.int32),
            pltpu.SMEM(block_scales.shape, F32),
            pltpu.VMEM(dest_factor.shape, F32),
            pltpu.VMEM(hour_factor.shape, F32),
            pltpu.SemaphoreType.DMA((hours,)),
            pltpu.SemaphoreType.DMA((3,)),
        ],
        compiler_params=pltpu.CompilerParams(vmem_limit_bytes=28 * 2**20),
        name="first",
    )(*[pltpu.with_memory_space_constraint(x, pltpu.HBM) for x in (counts, block_scales, dest_factor, hour_factor)])

    upper, lower = anchor_factor[:, :width], anchor_factor[:, width:]
    matrix, factor, part_factor = ((rank, rank), F32), ((rank, width), F32), ((rank, part_size), F32)
    for sweep in range(SWEEPS):
        near, far = sum_steps(message, "dst", 1)
        near_low, far_low = sum_steps(message_low, "dst", 1)
        if sweep == 0:
            flipped = call(flip_kernel, [((hours, cols, rows), BF16)], "flip", 4 * half_flops, tensor, near)
        upper, gram_part, gram, sent, kept = call(
            upper_kernel, [factor, matrix, matrix, ((rank, size), F32), ((rank, size), F32)],
            "upper", half_flops, tensor, upper, near, far, hour_gram, hour_t,
        )
        lower, sent_early = call(
            lower_kernel, [factor, part_factor], "lower", half_flops // 4,
            tensor, lower, near_low, far_low, gram_part, hour_t, sent, flipped,
        )
        received = swap(sent_early, "org", 1)
        sent_late = call(
            lower_late_kernel, [((anchor_rows, part_size), F32)], "lower_late", half_flops // 4,
            tensor, lower, hour_t, gram, sent,
        )
        received_late = swap(sent_late, "org", 1)
        kept, kept_late = call(
            lower_kept_kernel, [part_factor, ((anchor_rows, part_size), F32)], "lower_kept", half_flops // 2,
            tensor, lower, hour_t, kept, sent_late,
        )
        near, far = sum_steps(add(kept, received), "org", 2)
        near_late, far_late = sum_at_once(add(kept_late, received_late))
        late_own, gram_part = call(
            dest_late_kernel, [part_factor, matrix], "dest_late", 0, late_own, near_late, far_late, hour_gram
        )
        late_other = swap(late_own, "org", 1)
        dest_own = call(dest_kernel, [part_factor], "dest", 0, dest_own, near, far, gram_part)
        dest_other = swap(dest_own, "org", 1)
        if sweep + 1 < SWEEPS:
            parts = call(
                own_late_kernel, [factor, factor, matrix], "own_late", half_flops // 2, flipped, late_own, hour_t
            )
            parts = call(
                functools.partial(more_kernel, False, 0), [factor, factor, matrix], "own", half_flops // 2,
                flipped, dest_own, hour_t, *parts,
            )
            parts = call(
                functools.partial(more_kernel, True, 1), [factor, factor, matrix], "other_late", half_flops // 2,
                flipped, late_other, hour_t, *parts,
            )
            message = call(
                dest_upper_kernel, [((dest_rows, width), F32)], "dest_upper", half_flops // 4,
                flipped, dest_other, hour_t, parts[0], parts[2],
            )
            message_low = call(
                dest_lower_kernel, [factor], "dest_lower", half_flops // 4, flipped, dest_other, hour_t, parts[1]
            )
    anchor_now, dest_now = pl.pallas_call(
        store_own_kernel,
        in_specs=[WHOLE] * 4,
        out_specs=(ANYWHERE,) * 2,
        out_shape=(pltpu.HBM((rank, rows), F32), pltpu.HBM((rank, cols), F32)),
        scratch_shapes=[pltpu.SemaphoreType.DMA((4,))],
        compiler_params=PARAMS,
        name="store_own",
    )(*[in_vmem(x) for x in (upper, lower, dest_own, late_own)])
    dest_now = pl.pallas_call(
        store_other_kernel,
        in_specs=[WHOLE, WHOLE, ANYWHERE],
        out_specs=ANYWHERE,
        out_shape=pltpu.HBM((rank, cols), F32),
        scratch_shapes=[pltpu.SemaphoreType.DMA((2,))],
        input_output_aliases={2: 0},
        compiler_params=PARAMS,
        name="store_other",
    )(in_vmem(dest_other), in_vmem(late_other), pltpu.with_memory_space_constraint(dest_now, pltpu.HBM))
    return anchor_now, dest_now


def solution(mesh):
    return jax.shard_map(
        body,
        mesh=mesh,
        in_specs=(
            P(None, "org", "dst"),
            P(None, "org", "dst"),
            P(None, "org"),
            P(None, "dst"),
            P(),
        ),
        out_specs=(P(None, "org"), P(None, "dst")),
        check_vma=False,
    )
```

```python
import functools

import jax
import jax.numpy as jnp
from jax import lax
from jax.experimental import pallas as pl
from jax.experimental.pallas import tpu as pltpu
from jax.sharding import PartitionSpec as P

SCALE_BLOCK = 128
SWEEPS = 6
IN_FLIGHT = 4
HINT = 10**10
F32 = jnp.float32
BF16 = jnp.bfloat16

WHOLE = pl.BlockSpec(memory_space=pltpu.VMEM)
ANYWHERE = pl.BlockSpec(memory_space=pl.ANY)
PARAMS = pltpu.CompilerParams(vmem_limit_bytes=8 * 2**20)


def in_vmem(array):
    return pltpu.with_memory_space_constraint(array, pltpu.VMEM)


def gram_rows(rank, width):
    return 8 * -(-(rank // 8) // (width // rank))


def gram_cells(rank, width):
    per_row = width // rank
    for block in range(rank // 8):
        yield block, rank + 8 * (block // per_row), rank * (block % per_row)


def put_gram(message, gram):
    rank = gram.shape[0]
    width = message.shape[1]
    message[rank:, :] = jnp.zeros((message.shape[0] - rank, width), F32)
    for block, row, lane in gram_cells(rank, width):
        message[row : row + 8, lane : lane + rank] = gram[8 * block : 8 * block + 8, :]


def get_gram(message, rank):
    width = message.shape[1]
    return jnp.concatenate(
        [message[row : row + 8, lane : lane + rank] for _, row, lane in gram_cells(rank, width)], axis=0
    )


def parts_of(array):
    high = array.astype(BF16)
    return high, (array - high.astype(F32)).astype(BF16)


def own_gram(factor):
    def dot(left, right):
        return lax.dot_general(left, right, (((1,), (1,)), ((), ())), preferred_element_type=F32)

    high, low = parts_of(factor)
    return dot(high, high) + (dot(high, low) + dot(low, high))


def times(left, right):
    left_high, left_low = parts_of(left)
    right_high, right_low = parts_of(right)
    return jnp.dot(
        jnp.concatenate([left_high, left_low, left_high], axis=1),
        jnp.concatenate([right_high, right_high, right_low], axis=0),
        preferred_element_type=F32,
    )


def half(flip, size, part=None):
    core = lax.axis_index("org") % 2
    start = (1 - core if flip else core) * size
    if part is None:
        return pl.ds(pl.multiple_of(start, size), size)
    size //= 2
    return pl.ds(pl.multiple_of(start + part * size, size), size)


def hour_sum(parts, hour_t):
    total = None
    for hour, part in enumerate(parts):
        term = part * hour_t[:, hour : hour + 1]
        total = term if total is None else total + term
    return total


def first_kernel(
    counts, scales, dest, hour, tensor, message, message_low, dest_own, dest_late, hour_gram, hour_t,
    buffer, scale_now, dest_now, hour_now, arrived, small_arrived,
):
    hours, rows, cols = counts.shape
    small = [
        pltpu.make_async_copy(source, target, small_arrived.at[index])
        for index, (source, target) in enumerate(((scales, scale_now), (dest, dest_now), (hour, hour_now)))
    ]
    for copy in small:
        copy.start()
    large = [pltpu.make_async_copy(counts.at[h], buffer.at[h], arrived.at[h]) for h in range(hours)]
    for copy in large[:IN_FLIGHT]:
        copy.start()
    for copy in small:
        copy.wait()
    hour_t[...] = hour_now[...].T
    hour_gram[...] = own_gram(hour_t[...])
    dest_own[...] = dest_now[:, half(False, cols // 2, 0)]
    dest_late[...] = dest_now[:, half(False, cols // 2, 1)]
    dest_low = dest_now[...].astype(BF16)
    put_gram(message, own_gram(dest_now[...]))
    total = None
    for h in range(hours):
        large[h].wait()
        if h + IN_FLIGHT < hours:
            large[h + IN_FLIGHT].start()
        for row_block in range(rows // SCALE_BLOCK):
            row = pl.ds(row_block * SCALE_BLOCK, SCALE_BLOCK)
            scale = jnp.concatenate(
                [
                    jnp.full((1, SCALE_BLOCK), scale_now[h, row_block, col_block], F32)
                    for col_block in range(cols // SCALE_BLOCK)
                ],
                axis=1,
            )
            tensor[h, row, :] = (buffer[h, row, :].astype(F32) * scale).astype(BF16)
        part = lax.dot_general(dest_low, tensor[h], (((1,), (1,)), ((), ())), preferred_element_type=F32)
        part = part * hour_t[:, h : h + 1]
        total = part if total is None else total + part
    message[: total.shape[0], :] = total[:, : rows // 2]
    message_low[...] = total[:, rows // 2 :]


def flip_kernel(tensor, after, flipped):
    for h in range(tensor.shape[0]):
        flipped[h] = tensor[h].T


def store(copies, done):
    started = [
        pltpu.make_async_copy(source, target, done.at[index]) for index, (source, target) in enumerate(copies)
    ]
    for copy in started:
        copy.start()
    for copy in started:
        copy.wait()


def store_own_kernel(upper, lower, own, late, anchor_out, dest_out, done):
    width = upper.shape[1]
    size = 2 * own.shape[1]
    store(
        (
            (upper, anchor_out.at[:, pl.ds(0, width)]),
            (lower, anchor_out.at[:, pl.ds(width, width)]),
            (own, dest_out.at[:, half(False, size, 0)]),
            (late, dest_out.at[:, half(False, size, 1)]),
        ),
        done,
    )


def store_other_kernel(other, late, _, dest_out, done):
    size = 2 * other.shape[1]
    store(((other, dest_out.at[:, half(True, size, 0)]), (late, dest_out.at[:, half(True, size, 1)])), done)


def add_kernel(left, right, total):
    total[...] = left[...] + right[...]


def products(low, tensor, rows, cols, hour_t):
    return hour_sum(
        [jnp.dot(low, tensor[h, rows, cols], preferred_element_type=F32) for h in range(tensor.shape[0])], hour_t
    )


def updated(factor, totals, gram_part):
    return factor * totals / times(gram_part, factor)


def upper_kernel(tensor, anchor, near, far, hour_gram, hour_t, anchor_out, gram_part, gram, sent, kept):
    rank, width = anchor.shape
    message = near[...] + far[...]
    gram_part[...] = get_gram(message, rank) * hour_gram[...]
    anchor_out[...] = updated(anchor[...], message[:rank, :], gram_part[...])
    low = anchor_out[...].astype(BF16)
    size = tensor.shape[2] // 2
    sent[...] = products(low, tensor, pl.ds(0, width), half(True, size), hour_t)
    kept[...] = products(low, tensor, pl.ds(0, width), half(False, size), hour_t)
    gram[...] = own_gram(anchor_out[...])


def lower_kernel(tensor, anchor, near, far, gram_part, hour_t, before, _, anchor_out, sent):
    width = anchor.shape[1]
    anchor_out[...] = updated(anchor[...], near[...] + far[...], gram_part[...])
    low = anchor_out[...].astype(BF16)
    cols = half(True, tensor.shape[2] // 2, 0)
    sent[...] = before[:, : cols.size] + products(low, tensor, pl.ds(width, width), cols, hour_t)


def lower_late_kernel(tensor, anchor, hour_t, gram, before, sent):
    rank, width = anchor.shape
    low = anchor[...].astype(BF16)
    cols = half(True, tensor.shape[2] // 2, 1)
    sent[:rank, :] = before[:, cols.size :] + products(low, tensor, pl.ds(width, width), cols, hour_t)
    put_gram(sent, gram[...] + own_gram(anchor[...]))


def lower_kept_kernel(tensor, anchor, hour_t, before, sent, kept, kept_late):
    rank, width = anchor.shape
    low = anchor[...].astype(BF16)
    size = tensor.shape[2] // 2
    total = before[...] + products(low, tensor, pl.ds(width, width), half(False, size), hour_t)
    kept[...] = total[:, : size // 2]
    kept_late[:rank, :] = total[:, size // 2 :]
    kept_late[rank:, :] = sent[rank:, :]


def dest_late_kernel(dest, near, far, hour_gram, dest_out, gram_part):
    rank = dest.shape[0]
    message = near[...] + far[...]
    gram_part[...] = get_gram(message, rank) * hour_gram[...]
    dest_out[...] = updated(dest[...], message[:rank, :], gram_part[...])


def dest_kernel(dest, near, far, gram_part, dest_out):
    dest_out[...] = updated(dest[...], near[...] + far[...], gram_part[...])


def dest_products(dest, flipped, flip, part, width, index, hour_t):
    rows = half(flip, flipped.shape[1] // 2, part)
    return products(dest[...].astype(BF16), flipped, rows, pl.ds(index * width, width), hour_t)


def own_late_kernel(flipped, dest, hour_t, upper, lower, gram):
    width = upper.shape[1]
    upper[...] = dest_products(dest, flipped, False, 1, width, 0, hour_t)
    lower[...] = dest_products(dest, flipped, False, 1, width, 1, hour_t)
    gram[...] = own_gram(dest[...])


def more_kernel(flip, part, flipped, dest, hour_t, upper, lower, gram, upper_out, lower_out, gram_out):
    width = upper.shape[1]
    upper_out[...] = upper[...] + dest_products(dest, flipped, flip, part, width, 0, hour_t)
    lower_out[...] = lower[...] + dest_products(dest, flipped, flip, part, width, 1, hour_t)
    gram_out[...] = gram[...] + own_gram(dest[...])


def dest_upper_kernel(flipped, dest, hour_t, before, gram, message):
    rank, width = before.shape
    message[:rank, :] = before[...] + dest_products(dest, flipped, True, 0, width, 0, hour_t)
    put_gram(message, gram[...] + own_gram(dest[...]))


def dest_lower_kernel(flipped, dest, hour_t, before, message):
    message[...] = before[...] + dest_products(dest, flipped, True, 0, before.shape[1], 1, hour_t)


def call(kernel, outs, name, flops, *args):
    result = pl.pallas_call(
        kernel,
        in_specs=[WHOLE] * len(args),
        out_specs=tuple(WHOLE for _ in outs),
        out_shape=tuple(pltpu.VMEM(shape, dtype) for shape, dtype in outs),
        compiler_params=PARAMS,
        cost_estimate=pl.CostEstimate(flops=flops, bytes_accessed=0, transcendentals=0),
        name=name,
    )(*[in_vmem(arg) for arg in args])
    return result if len(outs) > 1 else result[0]


def swap(array, axis, mask):
    size = lax.axis_size(axis)
    return lax.ppermute(array, axis, [(index, index ^ mask) for index in range(size)])


def add(left, right):
    return call(add_kernel, [(left.shape, F32)], "add", HINT, left, right)


def masks(axis, first):
    size = lax.axis_size(axis)
    return [1 << bit for bit in range(size.bit_length() - 1) if 1 << bit >= first]


def far_first(axis):
    return [lax.axis_size(axis) - 1, *masks(axis, 1)[-2::-1]]


def sum_steps(message, axis, steps):
    for mask in steps[:-1]:
        message = add(message, swap(message, axis, mask))
    return message, swap(message, axis, steps[-1])


def sum_at_once(message):
    if lax.axis_size("org") != 8:
        return sum_steps(message, "org", masks("org", 2))
    return message + swap(message, "org", 2), swap(message, "org", 4) + swap(message, "org", 6)


def body(counts, block_scales, anchor_factor, dest_factor, hour_factor):
    hours, rows, cols = counts.shape
    rank = anchor_factor.shape[0]
    size = cols // 2
    width = rows // 2
    dest_rows = rank + gram_rows(rank, width)
    part_size = size // 2
    anchor_rows = rank + gram_rows(rank, part_size)
    half_flops = 2 * 4 * hours * rank * rows * size

    tensor, message, message_low, dest_own, late_own, hour_gram, hour_t = pl.pallas_call(
        first_kernel,
        in_specs=[ANYWHERE] * 4,
        out_specs=(WHOLE,) * 7,
        out_shape=(
            pltpu.VMEM((hours, rows, cols), BF16),
            pltpu.VMEM((dest_rows, width), F32),
            pltpu.VMEM((rank, width), F32),
            pltpu.VMEM((rank, part_size), F32),
            pltpu.VMEM((rank, part_size), F32),
            pltpu.VMEM((rank, rank), F32),
            pltpu.VMEM((rank, hours), F32),
        ),
        scratch_shapes=[
            pltpu.VMEM(counts.shape, jnp.int32),
            pltpu.SMEM(block_scales.shape, F32),
            pltpu.VMEM(dest_factor.shape, F32),
            pltpu.VMEM(hour_factor.shape, F32),
            pltpu.SemaphoreType.DMA((hours,)),
            pltpu.SemaphoreType.DMA((3,)),
        ],
        compiler_params=pltpu.CompilerParams(vmem_limit_bytes=28 * 2**20),
        name="first",
    )(*[pltpu.with_memory_space_constraint(x, pltpu.HBM) for x in (counts, block_scales, dest_factor, hour_factor)])

    upper, lower = anchor_factor[:, :width], anchor_factor[:, width:]
    matrix, factor, part_factor = ((rank, rank), F32), ((rank, width), F32), ((rank, part_size), F32)
    for sweep in range(SWEEPS):
        near, far = sum_steps(message, "dst", masks("dst", 1))
        near_low, far_low = sum_steps(message_low, "dst", far_first("dst"))
        if sweep == 0:
            flipped = call(flip_kernel, [((hours, cols, rows), BF16)], "flip", 4 * half_flops, tensor, near)
        upper, gram_part, gram, sent, kept = call(
            upper_kernel, [factor, matrix, matrix, ((rank, size), F32), ((rank, size), F32)],
            "upper", half_flops, tensor, upper, near, far, hour_gram, hour_t,
        )
        lower, sent_early = call(
            lower_kernel, [factor, part_factor], "lower", half_flops // 4,
            tensor, lower, near_low, far_low, gram_part, hour_t, sent, flipped,
        )
        received = swap(sent_early, "org", 1)
        sent_late = call(
            lower_late_kernel, [((anchor_rows, part_size), F32)], "lower_late", half_flops // 4,
            tensor, lower, hour_t, gram, sent,
        )
        received_late = swap(sent_late, "org", 1)
        kept, kept_late = call(
            lower_kept_kernel, [part_factor, ((anchor_rows, part_size), F32)], "lower_kept", half_flops // 2,
            tensor, lower, hour_t, kept, sent_late,
        )
        near, far = sum_steps(add(kept, received), "org", masks("org", 2))
        near_late, far_late = sum_at_once(add(kept_late, received_late))
        late_own, gram_part = call(
            dest_late_kernel, [part_factor, matrix], "dest_late", 0, late_own, near_late, far_late, hour_gram
        )
        late_other = swap(late_own, "org", 1)
        dest_own = call(dest_kernel, [part_factor], "dest", 0, dest_own, near, far, gram_part)
        dest_other = swap(dest_own, "org", 1)
        if sweep + 1 < SWEEPS:
            parts = call(
                own_late_kernel, [factor, factor, matrix], "own_late", half_flops // 2, flipped, late_own, hour_t
            )
            parts = call(
                functools.partial(more_kernel, False, 0), [factor, factor, matrix], "own", half_flops // 2,
                flipped, dest_own, hour_t, *parts,
            )
            parts = call(
                functools.partial(more_kernel, True, 1), [factor, factor, matrix], "other_late", half_flops // 2,
                flipped, late_other, hour_t, *parts,
            )
            message = call(
                dest_upper_kernel, [((dest_rows, width), F32)], "dest_upper", half_flops // 4,
                flipped, dest_other, hour_t, parts[0], parts[2],
            )
            message_low = call(
                dest_lower_kernel, [factor], "dest_lower", half_flops // 4, flipped, dest_other, hour_t, parts[1]
            )
    anchor_now, dest_now = pl.pallas_call(
        store_own_kernel,
        in_specs=[WHOLE] * 4,
        out_specs=(ANYWHERE,) * 2,
        out_shape=(pltpu.HBM((rank, rows), F32), pltpu.HBM((rank, cols), F32)),
        scratch_shapes=[pltpu.SemaphoreType.DMA((4,))],
        compiler_params=PARAMS,
        name="store_own",
    )(*[in_vmem(x) for x in (upper, lower, dest_own, late_own)])
    dest_now = pl.pallas_call(
        store_other_kernel,
        in_specs=[WHOLE, WHOLE, ANYWHERE],
        out_specs=ANYWHERE,
        out_shape=pltpu.HBM((rank, cols), F32),
        scratch_shapes=[pltpu.SemaphoreType.DMA((2,))],
        input_output_aliases={2: 0},
        compiler_params=PARAMS,
        name="store_other",
    )(in_vmem(dest_other), in_vmem(late_other), pltpu.with_memory_space_constraint(dest_now, pltpu.HBM))
    return anchor_now, dest_now


def solution(mesh):
    return jax.shard_map(
        body,
        mesh=mesh,
        in_specs=(
            P(None, "org", "dst"),
            P(None, "org", "dst"),
            P(None, "org"),
            P(None, "dst"),
            P(),
        ),
        out_specs=(P(None, "org"), P(None, "dst")),
        check_vma=False,
    )
```

```python
import functools

import jax
import jax.numpy as jnp
from jax import lax
from jax.experimental import pallas as pl
from jax.experimental.pallas import tpu as pltpu
from jax.sharding import PartitionSpec as P

SCALE_BLOCK = 128
SWEEPS = 6
IN_FLIGHT = 4
HINT = 10**10
F32 = jnp.float32
BF16 = jnp.bfloat16

WHOLE = pl.BlockSpec(memory_space=pltpu.VMEM)
ANYWHERE = pl.BlockSpec(memory_space=pl.ANY)
PARAMS = pltpu.CompilerParams(vmem_limit_bytes=8 * 2**20)


def in_vmem(array):
    return pltpu.with_memory_space_constraint(array, pltpu.VMEM)


def gram_rows(rank, width):
    return 8 * -(-(rank // 8) // (width // rank))


def gram_cells(rank, width):
    per_row = width // rank
    for block in range(rank // 8):
        yield block, rank + 8 * (block // per_row), rank * (block % per_row)


def put_gram(message, gram):
    rank = gram.shape[0]
    width = message.shape[1]
    message[rank:, :] = jnp.zeros((message.shape[0] - rank, width), F32)
    for block, row, lane in gram_cells(rank, width):
        message[row : row + 8, lane : lane + rank] = gram[8 * block : 8 * block + 8, :]


def get_gram(message, rank):
    width = message.shape[1]
    return jnp.concatenate(
        [message[row : row + 8, lane : lane + rank] for _, row, lane in gram_cells(rank, width)], axis=0
    )


def parts_of(array):
    high = array.astype(BF16)
    return high, (array - high.astype(F32)).astype(BF16)


def own_gram(factor):
    def dot(left, right):
        return lax.dot_general(left, right, (((1,), (1,)), ((), ())), preferred_element_type=F32)

    high, low = parts_of(factor)
    return dot(high, high) + (dot(high, low) + dot(low, high))


def times(left, right):
    left_high, left_low = parts_of(left)
    right_high, right_low = parts_of(right)
    return jnp.dot(
        jnp.concatenate([left_high, left_low, left_high], axis=1),
        jnp.concatenate([right_high, right_high, right_low], axis=0),
        preferred_element_type=F32,
    )


def half(flip, size, part=None):
    core = lax.axis_index("org") % 2
    start = (1 - core if flip else core) * size
    if part is None:
        return pl.ds(pl.multiple_of(start, size), size)
    size //= 2
    return pl.ds(pl.multiple_of(start + part * size, size), size)


def hour_sum(parts, hour_t):
    total = None
    for hour, part in enumerate(parts):
        term = part * hour_t[:, hour : hour + 1]
        total = term if total is None else total + term
    return total


def first_kernel(
    counts, scales, dest, hour, tensor, message, message_low, dest_own, dest_late, hour_gram, hour_t,
    buffer, scale_now, dest_now, hour_now, arrived, small_arrived,
):
    hours, rows, cols = counts.shape
    small = [
        pltpu.make_async_copy(source, target, small_arrived.at[index])
        for index, (source, target) in enumerate(((scales, scale_now), (dest, dest_now), (hour, hour_now)))
    ]
    for copy in small:
        copy.start()
    large = [pltpu.make_async_copy(counts.at[h], buffer.at[h], arrived.at[h]) for h in range(hours)]
    for copy in large[:IN_FLIGHT]:
        copy.start()
    for copy in small:
        copy.wait()
    hour_t[...] = hour_now[...].T
    hour_gram[...] = own_gram(hour_t[...])
    dest_own[...] = dest_now[:, half(False, cols // 2, 0)]
    dest_late[...] = dest_now[:, half(False, cols // 2, 1)]
    dest_low = dest_now[...].astype(BF16)
    put_gram(message, own_gram(dest_now[...]))
    total = None
    for h in range(hours):
        large[h].wait()
        if h + IN_FLIGHT < hours:
            large[h + IN_FLIGHT].start()
        for row_block in range(rows // SCALE_BLOCK):
            row = pl.ds(row_block * SCALE_BLOCK, SCALE_BLOCK)
            scale = jnp.concatenate(
                [
                    jnp.full((1, SCALE_BLOCK), scale_now[h, row_block, col_block], F32)
                    for col_block in range(cols // SCALE_BLOCK)
                ],
                axis=1,
            )
            tensor[h, row, :] = (buffer[h, row, :].astype(F32) * scale).astype(BF16)
        part = lax.dot_general(dest_low, tensor[h], (((1,), (1,)), ((), ())), preferred_element_type=F32)
        part = part * hour_t[:, h : h + 1]
        total = part if total is None else total + part
    message[: total.shape[0], :] = total[:, : rows // 2]
    message_low[...] = total[:, rows // 2 :]


def flip_kernel(tensor, after, flipped):
    for h in range(tensor.shape[0]):
        flipped[h] = tensor[h].T


def store(copies, done):
    started = [
        pltpu.make_async_copy(source, target, done.at[index]) for index, (source, target) in enumerate(copies)
    ]
    for copy in started:
        copy.start()
    for copy in started:
        copy.wait()


def store_own_kernel(upper, lower, own, late, anchor_out, dest_out, done):
    width = upper.shape[1]
    size = 2 * own.shape[1]
    store(
        (
            (upper, anchor_out.at[:, pl.ds(0, width)]),
            (lower, anchor_out.at[:, pl.ds(width, width)]),
            (own, dest_out.at[:, half(False, size, 0)]),
            (late, dest_out.at[:, half(False, size, 1)]),
        ),
        done,
    )


def store_other_kernel(other, late, _, dest_out, done):
    size = 2 * other.shape[1]
    store(((other, dest_out.at[:, half(True, size, 0)]), (late, dest_out.at[:, half(True, size, 1)])), done)


def add_kernel(left, right, total):
    total[...] = left[...] + right[...]


def products(low, tensor, rows, cols, hour_t):
    return hour_sum(
        [jnp.dot(low, tensor[h, rows, cols], preferred_element_type=F32) for h in range(tensor.shape[0])], hour_t
    )


def updated(factor, totals, gram_part):
    return factor * totals / times(gram_part, factor)


def upper_kernel(tensor, anchor, near, far, hour_gram, hour_t, anchor_out, gram_part, gram, sent, kept):
    rank, width = anchor.shape
    message = near[...] + far[...]
    gram_part[...] = get_gram(message, rank) * hour_gram[...]
    anchor_out[...] = updated(anchor[...], message[:rank, :], gram_part[...])
    low = anchor_out[...].astype(BF16)
    size = tensor.shape[2] // 2
    sent[...] = products(low, tensor, pl.ds(0, width), half(True, size), hour_t)
    kept[...] = products(low, tensor, pl.ds(0, width), half(False, size), hour_t)
    gram[...] = own_gram(anchor_out[...])


def lower_kernel(tensor, anchor, near, far, gram_part, hour_t, before, _, anchor_out, sent):
    width = anchor.shape[1]
    anchor_out[...] = updated(anchor[...], near[...] + far[...], gram_part[...])
    low = anchor_out[...].astype(BF16)
    cols = half(True, tensor.shape[2] // 2, 0)
    sent[...] = before[:, : cols.size] + products(low, tensor, pl.ds(width, width), cols, hour_t)


def lower_late_kernel(tensor, anchor, hour_t, gram, before, sent):
    rank, width = anchor.shape
    low = anchor[...].astype(BF16)
    cols = half(True, tensor.shape[2] // 2, 1)
    sent[:rank, :] = before[:, cols.size :] + products(low, tensor, pl.ds(width, width), cols, hour_t)
    put_gram(sent, gram[...] + own_gram(anchor[...]))


def lower_kept_kernel(tensor, anchor, hour_t, before, sent, kept, kept_late):
    rank, width = anchor.shape
    low = anchor[...].astype(BF16)
    size = tensor.shape[2] // 2
    total = before[...] + products(low, tensor, pl.ds(width, width), half(False, size), hour_t)
    kept[...] = total[:, : size // 2]
    kept_late[:rank, :] = total[:, size // 2 :]
    kept_late[rank:, :] = sent[rank:, :]


def dest_late_kernel(dest, near, far, hour_gram, dest_out, gram_part):
    rank = dest.shape[0]
    message = near[...] + far[...]
    gram_part[...] = get_gram(message, rank) * hour_gram[...]
    dest_out[...] = updated(dest[...], message[:rank, :], gram_part[...])


def dest_kernel(dest, near, far, gram_part, dest_out):
    dest_out[...] = updated(dest[...], near[...] + far[...], gram_part[...])


def dest_products(dest, flipped, flip, part, width, index, hour_t):
    rows = half(flip, flipped.shape[1] // 2, part)
    return products(dest[...].astype(BF16), flipped, rows, pl.ds(index * width, width), hour_t)


def own_late_kernel(flipped, dest, hour_t, upper, lower, gram):
    width = upper.shape[1]
    upper[...] = dest_products(dest, flipped, False, 1, width, 0, hour_t)
    lower[...] = dest_products(dest, flipped, False, 1, width, 1, hour_t)
    gram[...] = own_gram(dest[...])


def more_kernel(flip, part, flipped, dest, hour_t, upper, lower, gram, upper_out, lower_out, gram_out):
    width = upper.shape[1]
    upper_out[...] = upper[...] + dest_products(dest, flipped, flip, part, width, 0, hour_t)
    lower_out[...] = lower[...] + dest_products(dest, flipped, flip, part, width, 1, hour_t)
    gram_out[...] = gram[...] + own_gram(dest[...])


def dest_upper_kernel(flipped, dest, hour_t, before, gram, message):
    rank, width = before.shape
    message[:rank, :] = before[...] + dest_products(dest, flipped, True, 0, width, 0, hour_t)
    put_gram(message, gram[...] + own_gram(dest[...]))


def dest_lower_kernel(flipped, dest, hour_t, before, message):
    message[...] = before[...] + dest_products(dest, flipped, True, 0, before.shape[1], 1, hour_t)


def call(kernel, outs, name, flops, *args):
    result = pl.pallas_call(
        kernel,
        in_specs=[WHOLE] * len(args),
        out_specs=tuple(WHOLE for _ in outs),
        out_shape=tuple(pltpu.VMEM(shape, dtype) for shape, dtype in outs),
        compiler_params=PARAMS,
        cost_estimate=pl.CostEstimate(flops=flops, bytes_accessed=0, transcendentals=0),
        name=name,
    )(*[in_vmem(arg) for arg in args])
    return result if len(outs) > 1 else result[0]


def swap(array, axis, mask):
    size = lax.axis_size(axis)
    return lax.ppermute(array, axis, [(index, index ^ mask) for index in range(size)])


def add(left, right):
    return call(add_kernel, [(left.shape, F32)], "add", HINT, left, right)


def masks(axis, first):
    size = lax.axis_size(axis)
    return [1 << bit for bit in range(size.bit_length() - 1) if 1 << bit >= first]


def far_first(axis):
    return [lax.axis_size(axis) - 1, *masks(axis, 1)[-2::-1]]


def sum_steps(message, axis, steps):
    for mask in steps[:-1]:
        message = add(message, swap(message, axis, mask))
    return message, swap(message, axis, steps[-1])


def sum_at_once(message):
    if lax.axis_size("org") != 8:
        return sum_steps(message, "org", masks("org", 2))
    return message + swap(message, "org", 2), swap(message, "org", 4) + swap(message, "org", 6)


def body(counts, block_scales, anchor_factor, dest_factor, hour_factor):
    hours, rows, cols = counts.shape
    rank = anchor_factor.shape[0]
    size = cols // 2
    width = rows // 2
    dest_rows = rank + gram_rows(rank, width)
    part_size = size // 2
    anchor_rows = rank + gram_rows(rank, part_size)
    half_flops = 2 * 4 * hours * rank * rows * size

    tensor, message, message_low, dest_own, late_own, hour_gram, hour_t = pl.pallas_call(
        first_kernel,
        in_specs=[ANYWHERE] * 4,
        out_specs=(WHOLE,) * 7,
        out_shape=(
            pltpu.VMEM((hours, rows, cols), BF16),
            pltpu.VMEM((dest_rows, width), F32),
            pltpu.VMEM((rank, width), F32),
            pltpu.VMEM((rank, part_size), F32),
            pltpu.VMEM((rank, part_size), F32),
            pltpu.VMEM((rank, rank), F32),
            pltpu.VMEM((rank, hours), F32),
        ),
        scratch_shapes=[
            pltpu.VMEM(counts.shape, jnp.int32),
            pltpu.SMEM(block_scales.shape, F32),
            pltpu.VMEM(dest_factor.shape, F32),
            pltpu.VMEM(hour_factor.shape, F32),
            pltpu.SemaphoreType.DMA((hours,)),
            pltpu.SemaphoreType.DMA((3,)),
        ],
        compiler_params=pltpu.CompilerParams(vmem_limit_bytes=28 * 2**20),
        name="first",
    )(*[pltpu.with_memory_space_constraint(x, pltpu.HBM) for x in (counts, block_scales, dest_factor, hour_factor)])

    upper, lower = anchor_factor[:, :width], anchor_factor[:, width:]
    matrix, factor, part_factor = ((rank, rank), F32), ((rank, width), F32), ((rank, part_size), F32)
    for sweep in range(SWEEPS):
        steps = [masks("dst", 1), far_first("dst")]
        near, far = sum_steps(message, "dst", steps[sweep == 0])
        near_low, far_low = sum_steps(message_low, "dst", steps[sweep > 0])
        if sweep == 0:
            flipped = call(flip_kernel, [((hours, cols, rows), BF16)], "flip", 4 * half_flops, tensor, near)
        upper, gram_part, gram, sent, kept = call(
            upper_kernel, [factor, matrix, matrix, ((rank, size), F32), ((rank, size), F32)],
            "upper", half_flops, tensor, upper, near, far, hour_gram, hour_t,
        )
        lower, sent_early = call(
            lower_kernel, [factor, part_factor], "lower", half_flops // 4,
            tensor, lower, near_low, far_low, gram_part, hour_t, sent, flipped,
        )
        received = swap(sent_early, "org", 1)
        sent_late = call(
            lower_late_kernel, [((anchor_rows, part_size), F32)], "lower_late", half_flops // 4,
            tensor, lower, hour_t, gram, sent,
        )
        received_late = swap(sent_late, "org", 1)
        kept, kept_late = call(
            lower_kept_kernel, [part_factor, ((anchor_rows, part_size), F32)], "lower_kept", half_flops // 2,
            tensor, lower, hour_t, kept, sent_late,
        )
        near, far = sum_steps(add(kept, received), "org", masks("org", 2))
        near_late, far_late = sum_at_once(add(kept_late, received_late))
        late_own, gram_part = call(
            dest_late_kernel, [part_factor, matrix], "dest_late", 0, late_own, near_late, far_late, hour_gram
        )
        late_other = swap(late_own, "org", 1)
        dest_own = call(dest_kernel, [part_factor], "dest", 0, dest_own, near, far, gram_part)
        dest_other = swap(dest_own, "org", 1)
        if sweep + 1 < SWEEPS:
            parts = call(
                own_late_kernel, [factor, factor, matrix], "own_late", half_flops // 2, flipped, late_own, hour_t
            )
            parts = call(
                functools.partial(more_kernel, False, 0), [factor, factor, matrix], "own", half_flops // 2,
                flipped, dest_own, hour_t, *parts,
            )
            parts = call(
                functools.partial(more_kernel, True, 1), [factor, factor, matrix], "other_late", half_flops // 2,
                flipped, late_other, hour_t, *parts,
            )
            message = call(
                dest_upper_kernel, [((dest_rows, width), F32)], "dest_upper", half_flops // 4,
                flipped, dest_other, hour_t, parts[0], parts[2],
            )
            message_low = call(
                dest_lower_kernel, [factor], "dest_lower", half_flops // 4, flipped, dest_other, hour_t, parts[1]
            )
    anchor_now, dest_now = pl.pallas_call(
        store_own_kernel,
        in_specs=[WHOLE] * 4,
        out_specs=(ANYWHERE,) * 2,
        out_shape=(pltpu.HBM((rank, rows), F32), pltpu.HBM((rank, cols), F32)),
        scratch_shapes=[pltpu.SemaphoreType.DMA((4,))],
        compiler_params=PARAMS,
        name="store_own",
    )(*[in_vmem(x) for x in (upper, lower, dest_own, late_own)])
    dest_now = pl.pallas_call(
        store_other_kernel,
        in_specs=[WHOLE, WHOLE, ANYWHERE],
        out_specs=ANYWHERE,
        out_shape=pltpu.HBM((rank, cols), F32),
        scratch_shapes=[pltpu.SemaphoreType.DMA((2,))],
        input_output_aliases={2: 0},
        compiler_params=PARAMS,
        name="store_other",
    )(in_vmem(dest_other), in_vmem(late_other), pltpu.with_memory_space_constraint(dest_now, pltpu.HBM))
    return anchor_now, dest_now


def solution(mesh):
    return jax.shard_map(
        body,
        mesh=mesh,
        in_specs=(
            P(None, "org", "dst"),
            P(None, "org", "dst"),
            P(None, "org"),
            P(None, "dst"),
            P(),
        ),
        out_specs=(P(None, "org"), P(None, "dst")),
        check_vma=False,
    )
```
